256 devices in a mesh: dp: 4 (over x), fsdp: 64 (over z, y, core).
Axes of the slice: x: 4, y: 4, z: 8, core: 2. Of those that a mesh axis runs over, the one named last changes fastest.
Arguments:
- grad_query: bfloat16 [4, 4, 64, 192, 1536], P('dp', None, None, 'fsdp'), may hold values from -60 to 60
- grad_kv: bfloat16 [4, 4, 64, 256, 512], P('dp', None, None, 'fsdp'), may hold values from -60 to 60
- momentum_query: bfloat16 [4, 64, 2, 192, 1536], P('dp', 'fsdp'), may hold values from -120 to 120, as said below
- momentum_kv: bfloat16 [4, 64, 2, 256, 512], P('dp', 'fsdp'), may hold values from -120 to 120, as said below
- weight_query: float32 [4, 64, 192, 1536], P(None, 'dp', 'fsdp'), may hold values from -6 to 6
- weight_kv: float32 [4, 64, 256, 512], P(None, 'dp', 'fsdp'), may hold values from -6 to 6
- owner_query: int32 [4, 4, 16, 1], replicated, may hold values from 0 to 63; in each aligned block of 64 rows (0 to 63, 64 to 127, ..., all dimensions but the last counted through in order) at most 2 rows name the same one
- owner_kv: int32 [4, 4, 16, 1], replicated, may hold values from 0 to 63; in each aligned block of 64 rows (0 to 63, 64 to 127, ..., all dimensions but the last counted through in order) at most 2 rows name the same one
- max_logits: float32 [256, 4, 64], P(('dp', 'fsdp')), may hold values from 1 to 1500
Outputs:
- query_update: bfloat16 [4, 64, 192, 1536], P(None, 'dp', 'fsdp')
- kv_update: bfloat16 [4, 64, 256, 512], P(None, 'dp', 'fsdp')
- query_weight_new: float32 [4, 64, 192, 1536], P(None, 'dp', 'fsdp')
- kv_weight_new: float32 [4, 64, 256, 512], P(None, 'dp', 'fsdp')
- query_momentum_new: bfloat16 [4, 64, 2, 192, 1536], P('dp', 'fsdp')
- kv_momentum_new: bfloat16 [4, 64, 2, 256, 512], P('dp', 'fsdp')
The draws below stay inside these ranges and needn't reach their ends.
Inputs may be any that keep to these rules, and one draw needn't show every extreme that they name: `owner_query`: within one group's 4 * 16 blocks no owner has more than 2; in some group one owner has exactly 2. `owner_kv`: within one group's 4 * 16 blocks no owner has more than 2; in some group one owner has exactly 2. `momentum_query`: slots at or past an owner's number of blocks in the group are not read. `momentum_kv`: slots at or past an owner's number of blocks in the group are not read.
All inputs are finite; a program needn't handle non-finite values.
Results may differ from the reference program's by a relative error of at most 0.019.
Values may be sent and summed in bfloat16 or wider, within the bound.
No kernel may reach another device: no remote copies, remote signals or barrier semaphores. Data moves between devices by JAX's collectives and lax.ppermute only.
A program may use at most 64 MiB of HBM per device.

```python
import math
import jax
import jax.numpy as jnp
import numpy as np
from jax import lax

L = 4
H = 64
QN = 128
KN = 128
QL = 1536
KL = 512
STEPS = 5
QHD = 192
KVHD = 256
HD = 16
CAP = 2
SHARDS = 256
N_DP = 4
N_FSDP = 64


SPREAD_LOG = 1.1513


def spread_scales(key, outer, row_count, col_count):
    row_key, col_key = jax.random.split(key)
    row_scale = jnp.exp(jax.random.uniform(row_key, outer + (row_count, 1), jnp.float32, -SPREAD_LOG, SPREAD_LOG))
    col_scale = jnp.exp(jax.random.uniform(col_key, outer + (1, col_count), jnp.float32, -SPREAD_LOG, SPREAD_LOG))
    return row_scale * col_scale


def draw_grad_query(key, part):
    key = jax.random.fold_in(key, 11)
    scales = spread_scales(jax.random.fold_in(key, 1), (1, L, H), QHD, QL)
    shape = (N_DP, L, H, QHD, QL)
    values = jnp.clip(jax.random.normal(jax.random.fold_in(key, 2), shape, jnp.float32), -6.0, 6.0) * scales
    return values.astype(jnp.bfloat16)


def draw_grad_kv(key, part):
    key = jax.random.fold_in(key, 13)
    scales = spread_scales(jax.random.fold_in(key, 1), (1, L, H), KVHD, KL)
    shape = (N_DP, L, H, KVHD, KL)
    values = jnp.clip(jax.random.normal(jax.random.fold_in(key, 2), shape, jnp.float32), -6.0, 6.0) * scales
    return values.astype(jnp.bfloat16)


def draw_momentum_query(key, part):
    key = jax.random.fold_in(key, 17)
    scales = spread_scales(jax.random.fold_in(key, 1), (N_DP, N_FSDP, CAP), QHD, QL)
    shape = (N_DP, N_FSDP, CAP, QHD, QL)
    values = 2.0 * jnp.clip(jax.random.normal(jax.random.fold_in(key, 2), shape, jnp.float32), -6.0, 6.0) * scales
    return values.astype(jnp.bfloat16)


def draw_momentum_kv(key, part):
    key = jax.random.fold_in(key, 19)
    scales = spread_scales(jax.random.fold_in(key, 1), (N_DP, N_FSDP, CAP), KVHD, KL)
    shape = (N_DP, N_FSDP, CAP, KVHD, KL)
    values = 2.0 * jnp.clip(jax.random.normal(jax.random.fold_in(key, 2), shape, jnp.float32), -6.0, 6.0) * scales
    return values.astype(jnp.bfloat16)


def draw_max_logits(key, part):
    key = jax.random.fold_in(key, 41)
    level = jnp.exp(jax.random.uniform(jax.random.fold_in(key, 1), (1, L, H), jnp.float32, math.log(100.0), math.log(1500.0)))
    spread = jax.random.uniform(jax.random.fold_in(key, 2), (SHARDS, L, H), jnp.float32)
    return level * jnp.exp(-4.0 * spread ** 0.25)


def shard_levels(own_key, dims, pieces, smallest, high):
    def one(axis_at, blocks):
        heights = jax.random.uniform(jax.random.fold_in(jax.random.fold_in(own_key, 6), axis_at), (blocks,), jnp.float32, smallest / len(pieces), high / len(pieces))
        return jnp.repeat(jnp.exp(heights), dims[axis_at] // blocks).reshape((-1,) + (1,) * (len(dims) - axis_at - 1))

    gain = one(*pieces[0])
    for cut in pieces[1:]:
        gain = gain * one(*cut)
    return gain


def routed_block(stream_key, own, number, rows, number_of, top, bound, lean):
    sequence = jax.random.permutation(stream_key, number_of)
    packed, ordinary = load_shares(number_of, rows * top, bound, lean, True), load_shares(number_of, rows * top, bound, lean, False)
    places = jnp.arange(number_of)

    def named(tallies, turn):
        used = int((tallies > 0).sum())
        fixed = max(1, used // 4)
        passed = fixed + (places - fixed + turn * (used - fixed)) % max(1, number_of - fixed)
        return jnp.zeros((number_of,), jnp.int32).at[sequence[jnp.where(places < fixed, places, passed)]].set(jnp.asarray(tallies, jnp.int32))

    tallies = jnp.where(number % 4 == 0, named(packed, number // 4), named(ordinary, number - number // 4 - 1))
    mixed = jax.random.permutation(jax.random.fold_in(own, 3), number_of)
    giver, receiver = mixed[0:number_of // 2 * 2:2], mixed[1:number_of // 2 * 2:2]
    slack = jnp.minimum(tallies[giver] - 1, bound - tallies[receiver]) // 2
    slack = jnp.where((giver == sequence[0]) | (receiver == sequence[0]) | (tallies[receiver] == 0), 0, jnp.maximum(slack, 0))
    passed = jax.random.randint(jax.random.fold_in(own, 4), (number_of // 2,), 0, 1 << 20) % (slack + 1)
    tallies = tallies.at[giver].add(-passed).at[receiver].add(passed)
    members = jnp.searchsorted(jnp.cumsum(tallies), jnp.arange(rows * top), side="right").astype(jnp.int32)
    listing = members.reshape(top, rows).T
    listing = listing[jax.random.permutation(jax.random.fold_in(own, 1), rows)]
    turn = jax.random.randint(jax.random.fold_in(own, 2), (rows, 1), 0, top)
    return jnp.take_along_axis(listing, (jnp.arange(top)[None, :] + turn) % top, axis=1)


def load_shares(number_of, total, limit, slope, full):
    portions = [(1 << 20) // math.isqrt(grade ** slope) + 1 for grade in range(1, number_of + 1)]
    largest = limit if full else min(limit, max(-(-total // number_of), total * portions[0] // sum(portions)))
    least = 1 if total - largest >= number_of - 1 else 0
    given, surplus = [largest] + [least] * (number_of - 1), total - largest - least * (number_of - 1)
    while surplus > 0:
        candidates = [i for i in range(1, number_of) if given[i] < largest] or [i for i in range(1, number_of) if given[i] < limit]
        whole, left = sum([portions[i] for i in candidates]), surplus
        for i in candidates:
            addition = min(limit - given[i], max(1, left * portions[i] // whole), surplus)
            given[i] = given[i] + addition
            surplus = surplus - addition
    return np.array(given)


def scatter_about(own_key, shape, deviation, limit, shards=(), kind=jnp.bfloat16):
    factor_of = shard_levels(own_key, shape, shards, -0.22, 0.18) if shards else 1.0
    values = jax.random.normal(own_key, shape, jnp.float32) * deviation * factor_of
    return jnp.minimum(jnp.maximum(values, -limit), limit).astype(kind)


def setup_inputs(seed: int = 0) -> dict:
    seeds = jax.random.split(jax.random.key(seed), 10)
    grad_query = draw_grad_query(jax.random.fold_in(seeds[9], 71), 0)
    grad_kv = draw_grad_kv(jax.random.fold_in(seeds[9], 71), 0)
    momentum_query = draw_momentum_query(jax.random.fold_in(seeds[9], 71), 0)
    momentum_kv = draw_momentum_kv(jax.random.fold_in(seeds[9], 71), 0)
    weight_query = scatter_about(seeds[4], (L, H, QHD, QL), 1.0, 6.0, ((1, 4), (2, 64)), jnp.float32)
    weight_kv = scatter_about(seeds[5], (L, H, KVHD, KL), 1.0, 6.0, ((1, 4), (2, 64)), jnp.float32)
    owner_query_keys = jax.random.split(jax.random.fold_in(seeds[6], 1), N_DP * L * HD // (L * HD))
    owner_query_turns = jax.random.permutation(jax.random.fold_in(seeds[6], 3), N_DP * L * HD // (L * HD))
    owner_query = jax.vmap(lambda own, number: routed_block(jax.random.fold_in(seeds[6], 2), own, number, L * HD, N_FSDP, 1, CAP, 2))(owner_query_keys, owner_query_turns).reshape((N_DP, L, HD, 1))
    owner_kv_keys = jax.random.split(jax.random.fold_in(seeds[7], 1), N_DP * L * HD // (L * HD))
    owner_kv_turns = jax.random.permutation(jax.random.fold_in(seeds[7], 3), N_DP * L * HD // (L * HD))
    owner_kv = jax.vmap(lambda own, number: routed_block(jax.random.fold_in(seeds[7], 2), own, number, L * HD, N_FSDP, 1, CAP, 2))(owner_kv_keys, owner_kv_turns).reshape((N_DP, L, HD, 1))
    max_logits = draw_max_logits(jax.random.fold_in(seeds[9], 71), 0)
    return dict(grad_query=grad_query, grad_kv=grad_kv, momentum_query=momentum_query, momentum_kv=momentum_kv, weight_query=weight_query, weight_kv=weight_kv, owner_query=owner_query, owner_kv=owner_kv, max_logits=max_logits)


MOMENTUM_RATE = 0.95
LEARN_RATE = 0.02
DECAY_RATE = 0.1
CLIP_LEVEL = 100.0
NEWTON_FIRST = 3.4445
NEWTON_SECOND = -4.775
NEWTON_THIRD = 2.0315
EPSILON = 1e-07

def owner_slots(owners, node_count):
    hits = (owners[:, None] == jnp.arange(node_count, dtype=jnp.int32)[None, :]).astype(jnp.int32)
    before = jnp.cumsum(hits, axis=0) - hits
    return lax.optimization_barrier(jnp.sum(before * hits, axis=1)).astype(jnp.int32)

def newton_schulz(direction):
    scaled = direction / (jnp.sqrt(jnp.sum(direction * direction)) + EPSILON)
    for iteration in range(STEPS):
        square = jnp.dot(scaled, scaled.T, precision=lax.Precision.HIGHEST)
        polynomial = NEWTON_SECOND * square + NEWTON_THIRD * jnp.dot(square, square, precision=lax.Precision.HIGHEST)
        scaled = NEWTON_FIRST * scaled + jnp.dot(polynomial, scaled, precision=lax.Precision.HIGHEST)
    return scaled

def sum_partials(grads):
    summed = grads[0].astype(jnp.float32)
    for replica in range(1, N_DP):
        summed = summed + grads[replica].astype(jnp.float32)
    return summed.astype(jnp.bfloat16)

def by_group(full, row_count, col_count):
    shaped = full.reshape(L, N_DP, HD, row_count, col_count)
    return jnp.transpose(shaped, (1, 0, 2, 3, 4)).reshape(N_DP, L * HD, row_count, col_count)

def from_group(grouped, row_count, col_count):
    shaped = grouped.reshape(N_DP, L, HD, row_count, col_count)
    return jnp.transpose(shaped, (1, 0, 2, 3, 4)).reshape(L, H, row_count, col_count)

def optimize_kind(grads, momentum, owners):
    row_count = grads.shape[3]
    col_count = grads.shape[4]
    scale_factor = 0.2 * math.sqrt(max(row_count, col_count))
    reduced = by_group(sum_partials(grads), row_count, col_count)
    owner_flat = owners.reshape(N_DP, L * HD).astype(jnp.int32)
    slot_index = jax.vmap(lambda owned: owner_slots(owned, N_FSDP))(owner_flat)
    groups = jnp.broadcast_to(jnp.arange(N_DP, dtype=jnp.int32)[:, None], owner_flat.shape)
    previous = momentum[groups, owner_flat, slot_index]

    def one_block(gradient, earlier):
        gradient = gradient.astype(jnp.float32)
        carried = MOMENTUM_RATE * earlier.astype(jnp.float32) + gradient
        direction = gradient + MOMENTUM_RATE * carried
        orthogonal = newton_schulz(direction)
        return (carried.astype(jnp.bfloat16), (orthogonal * scale_factor).astype(jnp.bfloat16))

    def one_group(operands):
        return jax.vmap(one_block)(operands[0], operands[1])
    renewed, updates = lax.map(one_group, (reduced, previous))
    new_momentum = jnp.zeros(momentum.shape, jnp.bfloat16).at[groups, owner_flat, slot_index].set(renewed)
    return (from_group(updates, row_count, col_count), new_momentum)

def step_weights(weight, update, factor):
    stepped = weight - LEARN_RATE * (update.astype(jnp.float32) + DECAY_RATE * weight)
    return stepped * factor

def reference(grad_query, grad_kv, momentum_query, momentum_kv, weight_query, weight_kv, owner_query, owner_kv, max_logits):
    query_update, query_momentum_new = optimize_kind(grad_query, momentum_query, owner_query)
    kv_update, kv_momentum_new = optimize_kind(grad_kv, momentum_kv, owner_kv)
    peak = lax.optimization_barrier(jnp.max(max_logits, axis=0))
    shrink = jnp.minimum(1.0, CLIP_LEVEL / peak)
    root_shrink = jnp.sqrt(shrink)
    query_index = jnp.arange(QHD, dtype=jnp.int32)[None, None, :, None]
    query_factor = jnp.where(query_index < QN, root_shrink[:, :, None, None], shrink[:, :, None, None])
    kv_index = jnp.arange(KVHD, dtype=jnp.int32)[None, None, :, None]
    kv_factor = jnp.where(kv_index < KN, root_shrink[:, :, None, None], 1.0)
    query_weight_new = step_weights(weight_query, query_update, query_factor)
    kv_weight_new = step_weights(weight_kv, kv_update, kv_factor)
    return (query_update, kv_update, query_weight_new, kv_weight_new, query_momentum_new, kv_momentum_new)
```

```python
import math

import jax
import jax.numpy as jnp
from jax import lax
from jax.sharding import PartitionSpec as P

QN = 128
KN = 128
STEPS = 5


MOMENTUM_RATE = 0.95
LEARN_RATE = 0.02
DECAY_RATE = 0.1
CLIP_LEVEL = 100.0
NEWTON_FIRST = 3.4445
NEWTON_SECOND = -4.775
NEWTON_THIRD = 2.0315
EPSILON = 1e-07


def owner_slots(owners, node_count):
    hits = (owners[:, None] == jnp.arange(node_count, dtype=jnp.int32)[None, :]).astype(jnp.int32)
    before = jnp.cumsum(hits, axis=0) - hits
    return (jnp.sum(before * hits, axis=1), jnp.sum(hits, axis=0))


def dispatch_table(owners, node_count, capacity):
    slot_index, filled = owner_slots(owners, node_count)
    target = slot_index * node_count + owners
    dispatch = (
        jnp.arange(capacity * node_count, dtype=jnp.int32)[:, None] == target[None, :]
    ).astype(jnp.bfloat16)
    return (dispatch, filled)


def pack_slots(dispatch, grouped, node_count):
    matrices, row_count, col_count = grouped.shape
    packed = jnp.dot(
        dispatch,
        grouped.reshape(matrices, row_count * col_count),
        preferred_element_type=jnp.float32,
    )
    return packed.astype(jnp.bfloat16).reshape(
        dispatch.shape[0] // node_count, node_count * row_count, col_count
    )


def unpack_slots(dispatch, returned, node_count):
    capacity, total_rows, col_count = returned.shape
    row_count = total_rows // node_count
    flattened = returned.reshape(capacity * node_count, row_count * col_count)
    own_rows = lax.dot_general(
        dispatch, flattened, (((0,), (0,)), ((), ())), preferred_element_type=jnp.float32
    )
    return own_rows.astype(jnp.bfloat16).reshape(dispatch.shape[1], row_count, col_count)


def batched_newton(direction):
    frobenius = jnp.sqrt(jnp.sum(direction * direction, axis=(1, 2), keepdims=True))
    scaled = direction / (frobenius + EPSILON)
    for iteration in range(STEPS):
        square = jnp.einsum("sij,skj->sik", scaled, scaled, precision=lax.Precision.HIGHEST)
        polynomial = NEWTON_SECOND * square + NEWTON_THIRD * jnp.einsum(
            "sij,sjk->sik", square, square, precision=lax.Precision.HIGHEST
        )
        scaled = NEWTON_FIRST * scaled + jnp.einsum(
            "sij,sjk->sik", polynomial, scaled, precision=lax.Precision.HIGHEST
        )
    return scaled


def owner_step(arrived, previous, filled_here):
    capacity, row_count, col_count = arrived.shape
    in_use = (jnp.arange(capacity, dtype=jnp.int32) < filled_here)[:, None, None]
    gradient = arrived.astype(jnp.float32)
    carried = MOMENTUM_RATE * previous.astype(jnp.float32) + gradient
    direction = jnp.where(in_use, gradient + MOMENTUM_RATE * carried, 0.0)
    orthogonal = batched_newton(direction)
    scale_factor = 0.2 * math.sqrt(max(row_count, col_count))
    renewed = jnp.where(in_use, carried, 0.0).astype(jnp.bfloat16)
    return (renewed, (orthogonal * scale_factor).astype(jnp.bfloat16))


def step_weights(weight, update, factor):
    stepped = weight - LEARN_RATE * (update.astype(jnp.float32) + DECAY_RATE * weight)
    return stepped * factor


def on_device(
    grad_query,
    grad_kv,
    momentum_query,
    momentum_kv,
    weight_query,
    weight_kv,
    owner_query,
    owner_kv,
    max_logits,
):
    node_count = lax.axis_size("fsdp")
    group_count = lax.axis_size("dp")
    my_group = lax.axis_index("dp")
    my_node = lax.axis_index("fsdp")
    layers = grad_query.shape[1]
    head_count = grad_query.shape[2]
    per_group = head_count // group_count
    matrices = layers * per_group
    capacity = momentum_query.shape[2]
    query_rows = grad_query.shape[3]
    kv_rows = grad_kv.shape[3]
    query_cols = grad_query.shape[4]
    kv_cols = grad_kv.shape[4]
    all_query = owner_query.reshape(group_count, matrices)
    all_kv = owner_kv.reshape(group_count, matrices)
    query_owned = lax.dynamic_index_in_dim(all_query, my_group, 0, keepdims=False)
    kv_owned = lax.dynamic_index_in_dim(all_kv, my_group, 0, keepdims=False)
    query_dispatch, query_filled = dispatch_table(query_owned, node_count, capacity)
    kv_dispatch, kv_filled = dispatch_table(kv_owned, node_count, capacity)
    query_summed, kv_summed = (
        lax.psum_scatter(
            grad_query[0].astype(jnp.float32).astype(jnp.bfloat16),
            "dp",
            scatter_dimension=1,
            tiled=True,
        ).astype(jnp.float32),
        lax.psum_scatter(
            grad_kv[0].astype(jnp.float32).astype(jnp.bfloat16),
            "dp",
            scatter_dimension=1,
            tiled=True,
        ).astype(jnp.float32),
    )
    query_reduced = query_summed.astype(jnp.bfloat16).reshape(matrices, query_rows, query_cols)
    kv_reduced = kv_summed.astype(jnp.bfloat16).reshape(matrices, kv_rows, kv_cols)
    query_buckets = pack_slots(query_dispatch, query_reduced, node_count)
    kv_buckets = pack_slots(kv_dispatch, kv_reduced, node_count)
    query_arrived, kv_arrived = (
        lax.all_to_all(query_buckets, "fsdp", split_axis=1, concat_axis=1, tiled=True),
        lax.all_to_all(kv_buckets, "fsdp", split_axis=1, concat_axis=1, tiled=True),
    )
    query_count = lax.dynamic_index_in_dim(query_filled, my_node, 0, keepdims=False)
    kv_count = lax.dynamic_index_in_dim(kv_filled, my_node, 0, keepdims=False)
    query_renewed, query_outgoing = owner_step(query_arrived, momentum_query[0, 0], query_count)
    kv_renewed, kv_outgoing = owner_step(kv_arrived, momentum_kv[0, 0], kv_count)
    query_back, kv_back = (
        lax.all_to_all(query_outgoing, "fsdp", split_axis=1, concat_axis=1, tiled=True),
        lax.all_to_all(kv_outgoing, "fsdp", split_axis=1, concat_axis=1, tiled=True),
    )
    query_update = unpack_slots(query_dispatch, query_back, node_count).reshape(
        layers, per_group, query_rows, query_cols
    )
    kv_update = unpack_slots(kv_dispatch, kv_back, node_count).reshape(
        layers, per_group, kv_rows, kv_cols
    )
    merged = lax.pmax(max_logits, "dp")[0]
    group_peak = lax.dynamic_slice_in_dim(merged, my_group * per_group, per_group, 1)
    hop = 1
    while hop < node_count:
        pairs = [(i, (i + hop) % node_count) for i in range(node_count)]
        group_peak = jnp.maximum(group_peak, lax.ppermute(group_peak, "fsdp", pairs))
        hop *= 2
    shrink = jnp.minimum(1.0, CLIP_LEVEL / group_peak)
    root_shrink = jnp.sqrt(shrink)
    query_index = my_node * query_rows + jnp.arange(query_rows, dtype=jnp.int32)
    kv_index = my_node * kv_rows + jnp.arange(kv_rows, dtype=jnp.int32)
    query_factor = jnp.where(
        query_index[None, None, :, None] < QN,
        root_shrink[:, :, None, None],
        shrink[:, :, None, None],
    )
    kv_factor = jnp.where(kv_index[None, None, :, None] < KN, root_shrink[:, :, None, None], 1.0)
    query_weight_new = step_weights(weight_query, query_update, query_factor)
    kv_weight_new = step_weights(weight_kv, kv_update, kv_factor)
    return (
        query_update,
        kv_update,
        query_weight_new,
        kv_weight_new,
        query_renewed[None, None],
        kv_renewed[None, None],
    )


def solution(mesh):
    return jax.shard_map(
        on_device,
        mesh=mesh,
        in_specs=(
            P("dp", None, None, "fsdp", None),
            P("dp", None, None, "fsdp", None),
            P("dp", "fsdp", None, None, None),
            P("dp", "fsdp", None, None, None),
            P(None, "dp", "fsdp", None),
            P(None, "dp", "fsdp", None),
            P(),
            P(),
            P(("dp", "fsdp"), None, None),
        ),
        out_specs=(
            P(None, "dp", "fsdp", None),
            P(None, "dp", "fsdp", None),
            P(None, "dp", "fsdp", None),
            P(None, "dp", "fsdp", None),
            P("dp", "fsdp", None, None, None),
            P("dp", "fsdp", None, None, None),
        ),
        check_vma=False,
    )
```

```python
import math

import jax
import jax.numpy as jnp
from jax import lax
from jax.experimental import pallas as pl
from jax.experimental.pallas import tpu as pltpu
from jax.sharding import PartitionSpec as P

QN = 128
KN = 128
STEPS = 5
LAYERS = 4
HEADS = 64
GROUPS = 4
PER_GROUP = 16
NODES = 64
BLOCKS = 64
Q_ROWS, Q_COLS = 192, 1536
KV_ROWS, KV_COLS = 256, 512
Q_OWN, KV_OWN = Q_ROWS // NODES, KV_ROWS // NODES
LANE = 128
Q_TILES, KV_TILES = Q_COLS // LANE, KV_COLS // LANE
SUB = 8
MSG_COLS = 7
MSG = MSG_COLS * LANE
ROWS = NODES * SUB
PEAK_TILE = Q_OWN * Q_TILES + KV_OWN * KV_TILES
SPLIT = Q_OWN * Q_TILES // SUB
SPLIT_SUB = Q_OWN * Q_TILES % SUB

MOMENTUM_RATE = 0.95
LEARN_RATE = 0.02
DECAY_RATE = 0.1
CLIP_LEVEL = 100.0
NEWTON_FIRST = 3.4445
NEWTON_SECOND = -4.775
NEWTON_THIRD = 2.0315
EPSILON = 1e-07
Q_SCALE = 0.2 * math.sqrt(max(Q_ROWS, Q_COLS))
KV_SCALE = 0.2 * math.sqrt(max(KV_ROWS, KV_COLS))

F32 = jnp.float32
BF16 = jnp.bfloat16
I32 = jnp.int32
PARAMS = pltpu.CompilerParams(vmem_limit_bytes=48 * 1024 * 1024)


def place(tile):
    col, sub = divmod(tile, SUB)
    return slice(sub * BLOCKS, (sub + 1) * BLOCKS), slice(col * LANE, (col + 1) * LANE)


def tiles_of(kind):
    if kind == "q":
        return [(r, ct, r * Q_TILES + ct) for r in range(Q_OWN) for ct in range(Q_TILES)]
    base = Q_OWN * Q_TILES
    return [(r, ct, base + r * KV_TILES + ct) for r in range(KV_OWN) for ct in range(KV_TILES)]


def iota(shape, dim):
    return lax.broadcasted_iota(I32, shape, dim)


def dot(a, b):
    return jnp.dot(a, b, preferred_element_type=F32)


def dot_nt(a, b):
    return lax.dot_general(a, b, (((1,), (1,)), ((), ())), preferred_element_type=F32)


def one(cond):
    return jnp.where(cond, 1.0, 0.0).astype(BF16)


def pack_matrix():
    row, col = iota((ROWS, ROWS), 0), iota((ROWS, ROWS), 1)
    return one(((row >> 3) == (col & 63)) & ((row & 7) == (col >> 6)))


def unpack_matrix():
    row, col = iota((ROWS, ROWS), 0), iota((ROWS, ROWS), 1)
    return one(((row & 63) == (col >> 3)) & ((row >> 6) == (col & 7)))


def natural_matrix(own):
    size = own * NODES
    row, col = iota((size, size), 0), iota((size, size), 1)
    return one(row == (col & 63) * own + (col >> 6))


def split_matrix(own):
    size = own * NODES
    row, col = iota((size, size), 0), iota((size, size), 1)
    return one(col == (row & 63) * own + (row >> 6))


def to_message(q_natural, kv_natural, tiles_ref):
    q_split = dot(split_matrix(Q_OWN), q_natural).astype(BF16)
    kv_split = dot(split_matrix(KV_OWN), kv_natural).astype(BF16)
    tiles_ref[:, SPLIT * LANE :] = jnp.zeros((ROWS, MSG - SPLIT * LANE), BF16)
    for r, ct, tile in tiles_of("q"):
        rows, cols = place(tile)
        tiles_ref[rows, cols] = q_split[r * NODES : (r + 1) * NODES, ct * LANE : (ct + 1) * LANE]
    for r, ct, tile in tiles_of("kv"):
        rows, cols = place(tile)
        tiles_ref[rows, cols] = kv_split[r * NODES : (r + 1) * NODES, ct * LANE : (ct + 1) * LANE]
    return dot(pack_matrix(), tiles_ref[...])


def from_tiles(tiles, q_ref, kv_ref):
    for r, ct, tile in tiles_of("q"):
        rows, cols = place(tile)
        q_ref[r * NODES : (r + 1) * NODES, ct * LANE : (ct + 1) * LANE] = tiles[rows, cols]
    for r, ct, tile in tiles_of("kv"):
        rows, cols = place(tile)
        kv_ref[r * NODES : (r + 1) * NODES, ct * LANE : (ct + 1) * LANE] = tiles[rows, cols]
    return dot(natural_matrix(Q_OWN), q_ref[...]), dot(natural_matrix(KV_OWN), kv_ref[...])


def by_kind(q_matrix, kv_matrix, source, q_rows):
    edge = SPLIT * LANE
    q_part = dot(q_matrix, source[:, : edge + LANE])
    kv_part = dot(kv_matrix, source[:, edge:])
    mixed = jnp.where(q_rows, q_part[:, edge:], kv_part[:, :LANE])
    return jnp.concatenate([q_part[:, :edge], mixed, kv_part[:, LANE:]], axis=1)


def call(kernel, out_shape, *operands, **options):
    return pl.pallas_call(kernel, out_shape=out_shape, compiler_params=PARAMS, **options)(*operands)


def shape(dims, dtype):
    return jax.ShapeDtypeStruct(dims, dtype)


def arrange_kernel(q_ref, kv_ref, out_ref):
    out_ref[:, SPLIT * LANE :] = jnp.zeros((ROWS, MSG - SPLIT * LANE), BF16)
    for kind, ref in (("q", q_ref), ("kv", kv_ref)):
        for r, ct, tile in tiles_of(kind):
            rows, cols = place(tile)
            for layer in range(LAYERS):
                start = rows.start + layer * PER_GROUP
                out_ref[start : start + PER_GROUP, cols] = ref[layer, r, :, ct * LANE : (ct + 1) * LANE]


def arrange(grad_query, grad_kv):
    return call(
        arrange_kernel,
        shape((GROUPS * ROWS, MSG), BF16),
        grad_query,
        grad_kv,
        grid=(GROUPS,),
        in_specs=[
            pl.BlockSpec((LAYERS, Q_OWN, PER_GROUP, Q_COLS), lambda g: (0, 0, g, 0)),
            pl.BlockSpec((LAYERS, KV_OWN, PER_GROUP, KV_COLS), lambda g: (0, 0, g, 0)),
        ],
        out_specs=pl.BlockSpec((ROWS, MSG), lambda g: (g, 0)),
    )


def table_kernel(row_ref, col_ref, send_ref, late_ref, late_back_ref, back_ref, over_ref):
    owner_row = row_ref[...]
    owner_col = col_ref[...]
    down, across = iota((NODES, BLOCKS), 0), iota((NODES, BLOCKS), 1)

    def count(cond, axis):
        return jnp.sum(jnp.where(cond, 1.0, 0.0), axis=axis, keepdims=True)

    same = owner_col == owner_row
    slot_col = count(same & (across < down), 1)
    slot_row = count(same & (down < across), 0)
    hits = down == owner_row
    hits_back = owner_col == across
    fill_col, fill_row = count(hits, 1), count(hits_back, 0)
    over_col, over_row = slot_col > 0.5, slot_row > 0.5
    free_col, free_row = fill_col < 0.5, fill_row < 0.5
    over_rank_col, over_rank_row = count(over_row & (across < down), 1), count(over_col & (down < across), 0)
    free_rank_col, free_rank_row = count(free_row & (across < down), 1), count(free_col & (down < across), 0)

    late = hits & over_row
    send = (hits & ~over_row) | (free_col & over_row & (free_rank_col == over_rank_row))
    late_back = hits_back & over_col
    send_back = (hits_back & ~over_col) | (free_row & over_col & (free_rank_row == over_rank_col))

    def spread_rows(count_rows, per):
        return one((iota((count_rows, NODES), 0) >> per) == iota((count_rows, NODES), 1))

    def spread_cols(count_cols):
        return one(iota((BLOCKS, count_cols), 0) == (iota((BLOCKS, count_cols), 1) & 63))

    def to_peers(table):
        wide = dot(dot(spread_rows(ROWS, 3), one(table)).astype(BF16), spread_cols(ROWS))
        row, col = iota((ROWS, ROWS), 0), iota((ROWS, ROWS), 1)
        return jnp.where((row & 7) == (col >> 6), wide, 0.0).astype(BF16)

    def to_tiles(table, per):
        width = NODES << per
        mine = one((iota((ROWS, BLOCKS), 0) & 63) == iota((ROWS, BLOCKS), 1))
        peers = one(iota((NODES, width), 0) == (iota((NODES, width), 1) >> per))
        wide = dot(dot(mine, one(table)).astype(BF16), peers)
        row, col = iota((ROWS, width), 0), iota((ROWS, width), 1)
        return jnp.where((row >> 6) == (col & ((1 << per) - 1)), wide, 0.0).astype(BF16)

    send_ref[...] = to_peers(send)
    late_ref[...] = to_peers(late)
    late_back_ref[...] = to_tiles(late_back, 3)
    back_ref[...] = to_tiles(send_back, 4)
    over = jnp.where(over_col, 1.0, 0.0)
    for sub in range(SUB):
        over_ref[sub * BLOCKS : (sub + 1) * BLOCKS, :] = jnp.broadcast_to(over, (BLOCKS, LANE))


def tables(owners):
    return call(
        table_kernel,
        (
            shape((ROWS, ROWS), BF16),
            shape((ROWS, ROWS), BF16),
            shape((ROWS, ROWS), BF16),
            shape((ROWS, 2 * ROWS), BF16),
            shape((ROWS, LANE), F32),
        ),
        owners.reshape(1, BLOCKS),
        owners.reshape(BLOCKS, 1),
    )


def late_kernel(q_ref, kv_ref, out_ref, tiles_ref):
    out_ref[...] = to_message(q_ref[0, 0, 0], kv_ref[0, 0, 0], tiles_ref).astype(BF16)


def late_message(momentum_query, momentum_kv):
    return call(
        late_kernel,
        shape((ROWS, MSG), BF16),
        momentum_query,
        momentum_kv,
        grid=(1,),
        in_specs=[
            pl.BlockSpec((1, 1, 1, Q_ROWS, Q_COLS), lambda i: (0, 0, 1, 0, 0)),
            pl.BlockSpec((1, 1, 1, KV_ROWS, KV_COLS), lambda i: (0, 0, 1, 0, 0)),
        ],
        out_specs=pl.BlockSpec((ROWS, MSG), lambda i: (0, 0)),
        scratch_shapes=[pltpu.VMEM((ROWS, MSG), BF16)],
    )


def send_kernel(
    sum_ref, late_in_ref, q_send, q_late, q_late_back, q_over, kv_send, kv_late, kv_late_back, kv_over, peak_ref,
    out_ref, late_out_ref,
):
    row = iota((ROWS, LANE), 0)
    tile_rows = row < SPLIT_SUB * BLOCKS
    peer_rows = (row & 7) < SPLIT_SUB
    reduced = sum_ref[...].astype(F32)
    earlier = by_kind(q_late_back[...], kv_late_back[...], late_in_ref[...], tile_rows)
    carried = MOMENTUM_RATE * earlier + reduced
    direction = reduced + MOMENTUM_RATE * carried
    q_over_mask, kv_over_mask = q_over[...] > 0.5, kv_over[...] > 0.5
    columns = []
    for col in range(MSG_COLS):
        if col < SPLIT:
            mask = q_over_mask
        elif col == SPLIT:
            mask = jnp.where(tile_rows, q_over[...], kv_over[...]) > 0.5
        else:
            mask = kv_over_mask
        lanes = slice(col * LANE, (col + 1) * LANE)
        columns.append(jnp.where(mask, direction[:, lanes], reduced[:, lanes]))
    chosen = jnp.concatenate(columns, axis=1).astype(BF16)
    message = by_kind(q_send[...], kv_send[...], chosen, peer_rows)
    peak = peak_ref[...]
    high = peak.astype(BF16).astype(F32)
    middle = (peak - high).astype(BF16).astype(F32)
    low = (peak - high) - middle
    col, sub = divmod(PEAK_TILE, SUB)
    lane = iota((ROWS, LANE), 1)
    last = message[:, col * LANE :]
    first_half = lane < LANE // 2
    last = jnp.where((row & 7) == sub, jnp.where(first_half, high, middle), last)
    last = jnp.where((row & 7) == sub + 1, jnp.where(first_half, low, 0.0), last)
    out_ref[:, : col * LANE] = message[:, : col * LANE].astype(BF16)
    out_ref[:, col * LANE :] = last.astype(BF16)
    late_out_ref[...] = by_kind(q_late[...], kv_late[...], carried.astype(BF16), peer_rows).astype(BF16)


def halves(x):
    high = x.astype(BF16)
    return high, (x - high.astype(F32)).astype(BF16)


def product(a, b, op):
    return op(a[0], b[0]) + (op(a[0], b[1]) + op(a[1], b[0]))


def newton_step(x_ref):
    x = x_ref[...]
    parts = halves(x)
    square = product(parts, parts, dot_nt)
    square_parts = halves(square)
    polynomial = NEWTON_SECOND * square + NEWTON_THIRD * product(square_parts, square_parts, dot)
    x_ref[...] = NEWTON_FIRST * x + product(halves(polynomial), parts, dot)


def owner_kernel(
    used_ref, in_ref, q_mom, kv_mom, late_ref, out_ref, q_new, kv_new, factor_ref, q_x, kv_x, q_half, kv_half, tiles_ref,
    joined,
):
    received = dot(unpack_matrix(), in_ref[...])
    rows, cols = place(PEAK_TILE)
    top = received[rows, cols]
    rows, cols = place(PEAK_TILE + 1)
    bottom = received[rows, cols]
    peaks = jnp.max((top[:, :BLOCKS] + top[:, BLOCKS:]) + bottom[:, :BLOCKS], axis=0, keepdims=True)
    diagonal = iota((BLOCKS, BLOCKS), 0) == iota((BLOCKS, BLOCKS), 1)
    peak_col = jnp.sum(jnp.where(diagonal, jnp.broadcast_to(peaks, (BLOCKS, BLOCKS)), 0.0), axis=1, keepdims=True)
    shrink = jnp.minimum(1.0, CLIP_LEVEL / peak_col)
    factor_ref[0] = jnp.broadcast_to(jnp.sqrt(shrink), (BLOCKS, LANE))
    factor_ref[1] = jnp.broadcast_to(shrink, (BLOCKS, LANE))

    arrived = from_tiles(received.astype(BF16), q_half, kv_half)
    for kind, gradient, mom, new, x_ref in (
        (0, arrived[0], q_mom, q_new, q_x),
        (1, arrived[1], kv_mom, kv_new, kv_x),
    ):
        used = used_ref[kind] > 0
        carried = MOMENTUM_RATE * mom[0, 0, 0].astype(F32) + gradient
        new[0, 0, 0] = jnp.where(used, carried, 0.0).astype(BF16)
        direction = jnp.where(used, gradient + MOMENTUM_RATE * carried, gradient)
        norm = jnp.sqrt(jnp.sum(direction * direction)) + EPSILON
        x_ref[...] = direction / norm

    def body(_, carry):
        newton_step(q_x)
        newton_step(kv_x)
        return carry

    lax.fori_loop(0, STEPS, body, 0)
    outgoing = to_message((q_x[...] * Q_SCALE).astype(BF16), (kv_x[...] * KV_SCALE).astype(BF16), tiles_ref)
    joined[:, :SUB, :] = outgoing.reshape(NODES, SUB, MSG)
    joined[:, SUB:, :] = late_ref[...].astype(F32).reshape(NODES, SUB, MSG)
    out_ref[...] = joined[...].reshape(2 * ROWS, MSG).astype(BF16)


def owner_step(used, arrived, momentum_query, momentum_kv, late):
    whole = pl.BlockSpec((ROWS, MSG), lambda i: (0, 0))
    q_slot = pl.BlockSpec((1, 1, 1, Q_ROWS, Q_COLS), lambda i: (0, 0, 0, 0, 0))
    kv_slot = pl.BlockSpec((1, 1, 1, KV_ROWS, KV_COLS), lambda i: (0, 0, 0, 0, 0))
    return call(
        owner_kernel,
        (
            shape((2 * ROWS, MSG), BF16),
            shape((1, 1, 2, Q_ROWS, Q_COLS), BF16),
            shape((1, 1, 2, KV_ROWS, KV_COLS), BF16),
            shape((2, BLOCKS, LANE), F32),
        ),
        used,
        arrived,
        momentum_query,
        momentum_kv,
        late,
        grid=(1,),
        in_specs=[pl.BlockSpec(memory_space=pltpu.SMEM), whole, q_slot, kv_slot, whole],
        out_specs=[
            pl.BlockSpec((2 * ROWS, MSG), lambda i: (0, 0)),
            q_slot,
            kv_slot,
            pl.BlockSpec((2, BLOCKS, LANE), lambda i: (0, 0, 0)),
        ],
        scratch_shapes=[
            pltpu.VMEM((Q_ROWS, Q_COLS), F32),
            pltpu.VMEM((KV_ROWS, KV_COLS), F32),
            pltpu.VMEM((Q_ROWS, Q_COLS), BF16),
            pltpu.VMEM((KV_ROWS, KV_COLS), BF16),
            pltpu.VMEM((ROWS, MSG), BF16),
            pltpu.VMEM((NODES, 2 * SUB, MSG), F32),
        ],
    )


def finish_kernel(
    node_ref, in_ref, q_back, kv_back, factor_ref, weight_ref, q_old, kv_old,
    update_ref, weight_new, kv_update_ref, q_new, kv_new, q_half, kv_half,
):
    back = in_ref[...]
    row = iota((ROWS, LANE), 0)
    updates = by_kind(q_back[...], kv_back[...], back, row < SPLIT_SUB * BLOCKS)
    node = node_ref[0]
    for r in range(Q_OWN):
        factor = jnp.where(node * Q_OWN + r < QN, factor_ref[0], factor_ref[1]).reshape(LAYERS, PER_GROUP, LANE)
        for ct in range(Q_TILES):
            rows, cols = place(r * Q_TILES + ct)
            lanes = slice(ct * LANE, (ct + 1) * LANE)
            update = updates[rows, cols].reshape(LAYERS, PER_GROUP, LANE)
            update_ref[:, r, :, lanes] = update.astype(BF16)
            weight = weight_ref[:, r, :, lanes]
            weight_new[:, r, :, lanes] = (weight - LEARN_RATE * (update + DECAY_RATE * weight)) * factor
    for r, ct, tile in tiles_of("kv"):
        rows, cols = place(tile)
        kv_update_ref[r, :, ct * LANE : (ct + 1) * LANE] = updates[rows, cols].astype(BF16)
    wide_row, wide_col = iota((ROWS, 2 * ROWS), 0), iota((ROWS, 2 * ROWS), 1)
    late_matrix = one(((wide_row & 63) == (wide_col >> 4)) & ((wide_row >> 6) + SUB == (wide_col & 15)))
    late = dot(late_matrix, back).astype(BF16)
    q_late, kv_late = from_tiles(late, q_half, kv_half)
    q_new[0, 0, 0] = q_late.astype(BF16)
    kv_new[0, 0, 0] = kv_late.astype(BF16)


def finish(node, returned, q_back, kv_back, factors, weight_query, q_momentum, kv_momentum):
    def whole(*dims):
        return pl.BlockSpec(dims, lambda i: (0,) * len(dims))

    anywhere = pl.BlockSpec(memory_space=pl.ANY)
    q_dims = (LAYERS, Q_OWN, PER_GROUP, Q_COLS)
    kv_dims = (KV_OWN, BLOCKS, KV_COLS)
    return call(
        finish_kernel,
        (
            shape(q_dims, BF16),
            shape(q_dims, F32),
            shape(kv_dims, BF16),
            shape((1, 1, 2, Q_ROWS, Q_COLS), BF16),
            shape((1, 1, 2, KV_ROWS, KV_COLS), BF16),
        ),
        node,
        returned,
        q_back,
        kv_back,
        factors,
        weight_query,
        q_momentum,
        kv_momentum,
        grid=(1,),
        in_specs=[
            pl.BlockSpec(memory_space=pltpu.SMEM),
            whole(2 * ROWS, MSG),
            whole(ROWS, 2 * ROWS),
            whole(ROWS, 2 * ROWS),
            whole(2, BLOCKS, LANE),
            whole(*q_dims),
            anywhere,
            anywhere,
        ],
        out_specs=[
            whole(*q_dims),
            whole(*q_dims),
            whole(*kv_dims),
            pl.BlockSpec((1, 1, 1, Q_ROWS, Q_COLS), lambda i: (0, 0, 1, 0, 0)),
            pl.BlockSpec((1, 1, 1, KV_ROWS, KV_COLS), lambda i: (0, 0, 1, 0, 0)),
        ],
        scratch_shapes=[pltpu.VMEM((Q_ROWS, Q_COLS), BF16), pltpu.VMEM((KV_ROWS, KV_COLS), BF16)],
        input_output_aliases={6: 3, 7: 4},
    )


def exchange(message):
    return lax.all_to_all(message, "fsdp", split_axis=0, concat_axis=0, tiled=True)


def on_device(
    grad_query, grad_kv, momentum_query, momentum_kv, weight_query, weight_kv, owner_query, owner_kv, max_logits
):
    my_group = lax.axis_index("dp")
    my_node = lax.axis_index("fsdp")

    terms = arrange(jnp.transpose(grad_query[0], (0, 2, 1, 3)), jnp.transpose(grad_kv[0], (0, 2, 1, 3)))
    reduced = lax.psum_scatter(terms, "dp", scatter_dimension=0, tiled=True)

    peaks = lax.pmax(max_logits, "dp")[0]
    peaks = lax.dynamic_slice_in_dim(peaks, my_group * PER_GROUP, PER_GROUP, 1).reshape(1, BLOCKS)
    peaks = jnp.concatenate([peaks, peaks], axis=1)
    q_owners = lax.dynamic_index_in_dim(owner_query.reshape(GROUPS, BLOCKS), my_group, 0, keepdims=False)
    kv_owners = lax.dynamic_index_in_dim(owner_kv.reshape(GROUPS, BLOCKS), my_group, 0, keepdims=False)
    used = jnp.stack([jnp.any(q_owners == my_node), jnp.any(kv_owners == my_node)]).astype(I32)
    q_send, q_late, q_late_back, q_back, q_over = tables(q_owners)
    kv_send, kv_late, kv_late_back, kv_back, kv_over = tables(kv_owners)

    late_in = exchange(late_message(momentum_query, momentum_kv))
    message, late_out = call(
        send_kernel,
        (shape((ROWS, MSG), BF16), shape((ROWS, MSG), BF16)),
        reduced, late_in, q_send, q_late, q_late_back, q_over, kv_send, kv_late, kv_late_back, kv_over, peaks,
    )
    arrived = exchange(message)
    outgoing, q_momentum, kv_momentum, factors = owner_step(used, arrived, momentum_query, momentum_kv, late_out)
    returned = exchange(outgoing)
    q_update, q_weight, kv_update, q_momentum, kv_momentum = finish(
        my_node.astype(I32).reshape(1),
        returned,
        q_back,
        kv_back,
        factors,
        jnp.transpose(weight_query, (0, 2, 1, 3)),
        q_momentum,
        kv_momentum,
    )
    kv_update = jnp.transpose(kv_update.reshape(KV_OWN, LAYERS, PER_GROUP, KV_COLS), (1, 2, 0, 3))
    kv_index = my_node * KV_OWN + jnp.arange(KV_OWN, dtype=I32)
    root_shrink = factors[0, :, 0].reshape(LAYERS, PER_GROUP)
    kv_factor = jnp.where(kv_index[None, None, :, None] < KN, root_shrink[:, :, None, None], 1.0)
    kv_weight = (weight_kv - LEARN_RATE * (kv_update.astype(F32) + DECAY_RATE * weight_kv)) * kv_factor
    return (
        jnp.transpose(q_update, (0, 2, 1, 3)),
        kv_update,
        jnp.transpose(q_weight, (0, 2, 1, 3)),
        kv_weight,
        q_momentum,
        kv_momentum,
    )


def solution(mesh):
    return jax.shard_map(
        on_device,
        mesh=mesh,
        in_specs=(
            P("dp", None, None, "fsdp", None),
            P("dp", None, None, "fsdp", None),
            P("dp", "fsdp", None, None, None),
            P("dp", "fsdp", None, None, None),
            P(None, "dp", "fsdp", None),
            P(None, "dp", "fsdp", None),
            P(),
            P(),
            P(("dp", "fsdp"), None, None),
        ),
        out_specs=(
            P(None, "dp", "fsdp", None),
            P(None, "dp", "fsdp", None),
            P(None, "dp", "fsdp", None),
            P(None, "dp", "fsdp", None),
            P("dp", "fsdp", None, None, None),
            P("dp", "fsdp", None, None, None),
        ),
        check_vma=False,
    )
```

```python
import math

import jax
import jax.numpy as jnp
from jax import lax
from jax.experimental import pallas as pl
from jax.experimental.pallas import tpu as pltpu
from jax.sharding import PartitionSpec as P

QN = 128
KN = 128
STEPS = 5
LAYERS = 4
HEADS = 64
GROUPS = 4
PER_GROUP = 16
NODES = 64
BLOCKS = 64
Q_ROWS, Q_COLS = 192, 1536
KV_ROWS, KV_COLS = 256, 512
Q_OWN, KV_OWN = Q_ROWS // NODES, KV_ROWS // NODES
LANE = 128
Q_TILES, KV_TILES = Q_COLS // LANE, KV_COLS // LANE
SUB = 8
MSG_COLS = 7
MSG = MSG_COLS * LANE
ROWS = NODES * SUB
HALF = ROWS // 2
EXTRA = ROWS // 4
RING = ROWS - EXTRA
PEAK_TILE = Q_OWN * Q_TILES + KV_OWN * KV_TILES
SPLIT = Q_OWN * Q_TILES // SUB
SPLIT_SUB = Q_OWN * Q_TILES % SUB

MOMENTUM_RATE = 0.95
LEARN_RATE = 0.02
DECAY_RATE = 0.1
CLIP_LEVEL = 100.0
NEWTON_FIRST = 3.4445
NEWTON_SECOND = -4.775
NEWTON_THIRD = 2.0315
EPSILON = 1e-07
Q_SCALE = 0.2 * math.sqrt(max(Q_ROWS, Q_COLS))
KV_SCALE = 0.2 * math.sqrt(max(KV_ROWS, KV_COLS))

F32 = jnp.float32
BF16 = jnp.bfloat16
I32 = jnp.int32
PARAMS = pltpu.CompilerParams(vmem_limit_bytes=24 * 1024 * 1024)


def place(tile):
    col, sub = divmod(tile, SUB)
    return slice(sub * BLOCKS, (sub + 1) * BLOCKS), slice(col * LANE, (col + 1) * LANE)


def tiles_of(kind):
    if kind == "q":
        return [(r, ct, r * Q_TILES + ct) for r in range(Q_OWN) for ct in range(Q_TILES)]
    base = Q_OWN * Q_TILES
    return [(r, ct, base + r * KV_TILES + ct) for r in range(KV_OWN) for ct in range(KV_TILES)]


def in_hbm(x):
    return pltpu.with_memory_space_constraint(x, pltpu.HBM)


def iota(shape, dim):
    return lax.broadcasted_iota(I32, shape, dim)


def dot(a, b):
    return jnp.dot(a, b, preferred_element_type=F32)


def dot_nt(a, b):
    return lax.dot_general(a, b, (((1,), (1,)), ((), ())), preferred_element_type=F32)


def one(cond):
    return jnp.where(cond, 1.0, 0.0).astype(BF16)


def pack_matrix():
    row, col = iota((ROWS, ROWS), 0), iota((ROWS, ROWS), 1)
    return one(((row >> 3) == (col & 63)) & ((row & 7) == (col >> 6)))


def unpack_matrix():
    row, col = iota((ROWS, ROWS), 0), iota((ROWS, ROWS), 1)
    return one(((row & 63) == (col >> 3)) & ((row >> 6) == (col & 7)))


def natural_matrix(own):
    size = own * NODES
    row, col = iota((size, size), 0), iota((size, size), 1)
    return one(row == (col & 63) * own + (col >> 6))


def split_matrix(own):
    size = own * NODES
    row, col = iota((size, size), 0), iota((size, size), 1)
    return one(col == (row & 63) * own + (row >> 6))


def to_message(q_natural, kv_natural, tiles_ref):
    q_split = dot(split_matrix(Q_OWN), q_natural).astype(BF16)
    kv_split = dot(split_matrix(KV_OWN), kv_natural).astype(BF16)
    tiles_ref[:, SPLIT * LANE :] = jnp.zeros((ROWS, MSG - SPLIT * LANE), BF16)
    for r, ct, tile in tiles_of("q"):
        rows, cols = place(tile)
        tiles_ref[rows, cols] = q_split[r * NODES : (r + 1) * NODES, ct * LANE : (ct + 1) * LANE]
    for r, ct, tile in tiles_of("kv"):
        rows, cols = place(tile)
        tiles_ref[rows, cols] = kv_split[r * NODES : (r + 1) * NODES, ct * LANE : (ct + 1) * LANE]
    return dot(pack_matrix(), tiles_ref[...])


def from_tiles(tiles, q_ref, kv_ref):
    for r, ct, tile in tiles_of("q"):
        rows, cols = place(tile)
        q_ref[r * NODES : (r + 1) * NODES, ct * LANE : (ct + 1) * LANE] = tiles[rows, cols]
    for r, ct, tile in tiles_of("kv"):
        rows, cols = place(tile)
        kv_ref[r * NODES : (r + 1) * NODES, ct * LANE : (ct + 1) * LANE] = tiles[rows, cols]
    return dot(natural_matrix(Q_OWN), q_ref[...]), dot(natural_matrix(KV_OWN), kv_ref[...])


def by_kind(q_matrix, kv_matrix, source, q_rows):
    edge = SPLIT * LANE
    q_part = dot(q_matrix, source[:, : edge + LANE])
    kv_part = dot(kv_matrix, source[:, edge:])
    mixed = jnp.where(q_rows, q_part[:, edge:], kv_part[:, :LANE])
    return jnp.concatenate([q_part[:, :edge], mixed, kv_part[:, LANE:]], axis=1)


def call(kernel, out_shape, *operands, **options):
    return pl.pallas_call(kernel, out_shape=out_shape, compiler_params=PARAMS, **options)(*operands)


def whole(*dims):
    return pl.BlockSpec(dims, lambda i: (0,) * len(dims))


def shape(dims, dtype):
    return jax.ShapeDtypeStruct(dims, dtype)


def parts_of(value):
    high = value.astype(BF16).astype(F32)
    middle = (value - high).astype(BF16).astype(F32)
    return high, middle, (value - high) - middle


def peak_tile(column):
    high, middle, low = parts_of(column)
    lane = iota((column.shape[0], LANE), 1)
    return jnp.where(lane == 0, high, jnp.where(lane == 1, middle, jnp.where(lane == 2, low, 0.0))).astype(BF16)


def peak_column(tile):
    lane = iota(tile.shape, 1)
    return jnp.sum(jnp.where(lane < 3, tile.astype(F32), 0.0), axis=1, keepdims=True)


def group_tiles(group, q_ref, kv_ref, peak_ref, put):
    for tile in range(PEAK_TILE + 1, MSG_COLS * SUB):
        rows, cols = place(tile)
        put(rows.start, cols, jnp.zeros((BLOCKS, LANE), BF16))
    rows, cols = place(PEAK_TILE)
    for layer in range(LAYERS):
        spread = jnp.broadcast_to(peak_ref[layer : layer + 1, :], (PER_GROUP, HEADS))
        mine = iota((PER_GROUP, HEADS), 1) == iota((PER_GROUP, HEADS), 0) + group * PER_GROUP
        column = jnp.sum(jnp.where(mine, spread, 0.0), axis=1, keepdims=True)
        put(rows.start + layer * PER_GROUP, cols, peak_tile(column))
    for kind, ref in (("q", q_ref), ("kv", kv_ref)):
        for r, ct, tile in tiles_of(kind):
            rows, cols = place(tile)
            for layer in range(LAYERS):
                put(rows.start + layer * PER_GROUP, cols, ref[layer, r, :, ct * LANE : (ct + 1) * LANE])


def window(start, size):
    return slice(start, start + size)


def first_kernel(
    group_ref, q_far, kv_far, q_next, kv_next, q_last, kv_last, peak_ref, forward_out, backward_out
):
    def put_far(start, cols, value):
        out = (forward_out, backward_out)[start // HALF]
        out[window(start % HALF, value.shape[0]), cols] = value

    def put_next(start, cols, value):
        if start >= ROWS - EXTRA:
            forward_out[window(start - ROWS + EXTRA + HALF, value.shape[0]), cols] = value

    def put_last(start, cols, value):
        if start < EXTRA:
            backward_out[window(start + HALF, value.shape[0]), cols] = value

    group_tiles(group_ref[0], q_far, kv_far, peak_ref, put_far)
    group_tiles(group_ref[1], q_next, kv_next, peak_ref, put_next)
    group_tiles(group_ref[2], q_last, kv_last, peak_ref, put_last)


def mine_kernel(group_ref, q_ref, kv_ref, peak_ref, out_ref):
    def put(start, cols, value):
        out_ref[window(start, value.shape[0]), cols] = value

    group_tiles(group_ref[0], q_ref, kv_ref, peak_ref, put)


def combine_kernel(
    group_ref, q_next, kv_next, q_last, kv_last, peak_ref, from_last, from_next, next_out, last_out
):
    def put_next(start, cols, value):
        if start >= ROWS - EXTRA:
            return
        if start < HALF:
            value = (value.astype(F32) + from_last[window(start, value.shape[0]), cols].astype(F32)).astype(BF16)
        next_out[window(start, value.shape[0]), cols] = value

    def put_last(start, cols, value):
        if start < EXTRA:
            return
        here = window(start - EXTRA, value.shape[0])
        if start >= HALF:
            far = from_next[window(start - HALF, value.shape[0]), cols]
            if window(start // BLOCKS * BLOCKS, BLOCKS) == peak_rows and cols == peak_cols:
                value = peak_tile(jnp.maximum(peak_column(value), peak_column(far)))
            else:
                value = (value.astype(F32) + far.astype(F32)).astype(BF16)
        last_out[here, cols] = value

    peak_rows, peak_cols = place(PEAK_TILE)
    group_tiles(group_ref[0], q_next, kv_next, peak_ref, put_next)
    group_tiles(group_ref[1], q_last, kv_last, peak_ref, put_last)


def arrange_call(kernel, groups, grad_query, grad_kv, peaks, extra, out_shape, hint=None):
    count = groups.shape[0]

    def at(index):
        return [
            pl.BlockSpec((LAYERS, Q_OWN, PER_GROUP, Q_COLS), lambda i, g: (0, 0, g[index], 0)),
            pl.BlockSpec((LAYERS, KV_OWN, PER_GROUP, KV_COLS), lambda i, g: (0, 0, g[index], 0)),
        ]

    def all_of(x):
        return pl.BlockSpec(x.shape, lambda i, g: (0,) * len(x.shape))

    return pl.pallas_call(
        kernel,
        out_shape=out_shape,
        grid_spec=pltpu.PrefetchScalarGridSpec(
            num_scalar_prefetch=1,
            grid=(1,),
            in_specs=sum([at(index) for index in range(count)], []) + [all_of(x) for x in (peaks, *extra)],
            out_specs=[all_of(x) for x in out_shape],
        ),
        compiler_params=PARAMS,
        cost_estimate=hint,
    )(groups, *([in_hbm(grad_query), grad_kv] * count), peaks, *extra)


SEND, LATE, SEND_BACK, LATE_BACK = range(4)


def table_kernel(group_ref, q_ref, kv_ref, table_ref, over_ref, fill_ref):
    group = group_ref[0]
    down, across = iota((NODES, BLOCKS), 0), iota((NODES, BLOCKS), 1)

    def count(cond, axis):
        return jnp.sum(jnp.where(cond, 1.0, 0.0), axis=axis, keepdims=True)

    for kind, ref in enumerate((q_ref, kv_ref)):
        owner_row = jnp.zeros((SUB, BLOCKS), F32)
        for layer in range(LAYERS):
            piece = jnp.broadcast_to(ref[group, layer].astype(F32), (SUB, PER_GROUP)).astype(BF16)
            spot = iota((PER_GROUP, BLOCKS), 1) == iota((PER_GROUP, BLOCKS), 0) + layer * PER_GROUP
            owner_row += dot(piece, one(spot))
        owner_row = owner_row[:1].astype(I32)
        spread = jnp.broadcast_to(owner_row, (BLOCKS, BLOCKS))
        owner_col = jnp.sum(jnp.where(down == across, spread, 0).astype(F32), axis=1, keepdims=True).astype(I32)
        same = owner_col == owner_row
        slot_col = count(same & (across < down), 1)
        slot_row = count(same & (down < across), 0)
        hits = down == owner_row
        hits_back = owner_col == across
        fill_col, fill_row = count(hits, 1), count(hits_back, 0)
        over_col, over_row = slot_col > 0.5, slot_row > 0.5
        free_col, free_row = fill_col < 0.5, fill_row < 0.5
        over_rank_col, over_rank_row = count(over_row & (across < down), 1), count(over_col & (down < across), 0)
        free_rank_col, free_rank_row = count(free_row & (across < down), 1), count(free_col & (down < across), 0)
        table_ref[kind, SEND] = one(
            (hits & ~over_row) | (free_col & over_row & (free_rank_col == over_rank_row))
        )
        table_ref[kind, LATE] = one(hits & over_row)
        table_ref[kind, SEND_BACK] = one(
            (hits_back & ~over_col) | (free_row & over_col & (free_rank_row == over_rank_col))
        )
        table_ref[kind, LATE_BACK] = one(hits_back & over_col)
        over_ref[kind] = jnp.broadcast_to(jnp.where(over_col, 1.0, 0.0), (BLOCKS, LANE))
        fill_ref[kind] = jnp.broadcast_to(fill_col, (BLOCKS, LANE))


def tables(group, owner_query, owner_kv):
    return call(
        table_kernel,
        (shape((2, 4, NODES, BLOCKS), BF16), shape((2, BLOCKS, LANE), F32), shape((2, NODES, LANE), F32)),
        group,
        jnp.transpose(owner_query, (0, 1, 3, 2)),
        jnp.transpose(owner_kv, (0, 1, 3, 2)),
        in_specs=[pl.BlockSpec(memory_space=pltpu.SMEM)] + [pl.BlockSpec(memory_space=pltpu.VMEM)] * 2,
    )


def to_peers(table):
    rows = one((iota((ROWS, NODES), 0) >> 3) == iota((ROWS, NODES), 1))
    cols = one(iota((BLOCKS, ROWS), 0) == (iota((BLOCKS, ROWS), 1) & 63))
    wide = dot(dot(rows, table).astype(BF16), cols)
    row, col = iota((ROWS, ROWS), 0), iota((ROWS, ROWS), 1)
    return jnp.where((row & 7) == (col >> 6), wide, 0.0).astype(BF16)


def to_tiles(table):
    rows = one((iota((ROWS, BLOCKS), 0) & 63) == iota((ROWS, BLOCKS), 1))
    cols = one(iota((NODES, ROWS), 0) == (iota((NODES, ROWS), 1) >> 3))
    wide = dot(dot(rows, table).astype(BF16), cols)
    row, col = iota((ROWS, ROWS), 0), iota((ROWS, ROWS), 1)
    return jnp.where((row >> 6) == (col & 7), wide, 0.0).astype(BF16)


def late_kernel(q_ref, kv_ref, out_ref, tiles_ref):
    out_ref[...] = to_message(q_ref[0, 0, 0], kv_ref[0, 0, 0], tiles_ref).astype(BF16)


def late_message(momentum_query, momentum_kv):
    return call(
        late_kernel,
        pltpu.HBM((ROWS, MSG), BF16),
        in_hbm(momentum_query),
        in_hbm(momentum_kv),
        grid=(1,),
        in_specs=[
            pl.BlockSpec((1, 1, 1, Q_ROWS, Q_COLS), lambda i: (0, 0, 1, 0, 0)),
            pl.BlockSpec((1, 1, 1, KV_ROWS, KV_COLS), lambda i: (0, 0, 1, 0, 0)),
        ],
        out_specs=pl.BlockSpec((ROWS, MSG), lambda i: (0, 0)),
        scratch_shapes=[pltpu.VMEM((ROWS, MSG), BF16)],
    )


def earlier_kernel(late_in_ref, table_ref, out_ref):
    tile_rows = iota((ROWS, LANE), 0) < SPLIT_SUB * BLOCKS
    q_matrix, kv_matrix = to_tiles(table_ref[0, LATE_BACK]), to_tiles(table_ref[1, LATE_BACK])
    out_ref[...] = by_kind(q_matrix, kv_matrix, late_in_ref[...], tile_rows).astype(BF16)


def send_kernel(
    mine_ref, last_ref, next_ref, first_last, first_next, earlier_ref, table_ref, over_ref, out_hbm, carried_hbm,
    chosen, carried, message, sems,
):
    row = iota((ROWS, LANE), 0)
    q_over = jnp.concatenate([over_ref[0]] * SUB, axis=0)
    kv_over = jnp.concatenate([over_ref[1]] * SUB, axis=0)
    for col in range(MSG_COLS):
        lanes = slice(col * LANE, (col + 1) * LANE)
        last = jnp.concatenate([last_ref[:, lanes], first_last[HALF:, lanes]], axis=0).astype(F32)
        following = jnp.concatenate([first_next[HALF:, lanes], next_ref[:, lanes]], axis=0).astype(F32)
        reduced = mine_ref[:, lanes].astype(F32) + (last + following)
        reduced = reduced.astype(BF16).astype(F32)
        moved = MOMENTUM_RATE * earlier_ref[:, lanes].astype(F32) + reduced
        carried[:, lanes] = moved.astype(BF16)
        if col < SPLIT:
            mask = q_over
        elif col == SPLIT:
            mask = jnp.where(row < SPLIT_SUB * BLOCKS, q_over, kv_over)
        else:
            mask = kv_over
        chosen[:, lanes] = jnp.where(mask > 0.5, reduced + MOMENTUM_RATE * moved, reduced).astype(BF16)
    carried_copy = pltpu.make_async_copy(carried, carried_hbm, sems.at[0])
    carried_copy.start()
    edge = SPLIT * LANE
    q_part = dot(to_peers(table_ref[0, SEND]), chosen[:, : edge + LANE])
    message[:, :edge] = q_part[:, :edge].astype(BF16)
    q_copy = pltpu.make_async_copy(message.at[:, :edge], out_hbm.at[:, :edge], sems.at[1])
    q_copy.start()
    kv_part = dot(to_peers(table_ref[1, SEND]), chosen[:, edge:])
    peer_rows = (row & 7) < SPLIT_SUB
    message[:, edge : edge + LANE] = jnp.where(peer_rows, q_part[:, edge:], kv_part[:, :LANE]).astype(BF16)
    rows, cols = place(PEAK_TILE)
    peak = jnp.maximum(peak_column(mine_ref[rows, cols]), peak_column(last_ref[rows, cols]))
    peak = jnp.maximum(peak, peak_column(next_ref[rows.start - EXTRA : rows.stop - EXTRA, cols]))
    spot = iota((BLOCKS, LANE), 0) == (iota((BLOCKS, LANE), 1) & 63)
    peak = jnp.sum(jnp.where(spot, jnp.broadcast_to(peak, (BLOCKS, LANE)), 0.0), axis=0, keepdims=True)
    high, middle, low = parts_of(peak)
    sub = PEAK_TILE % SUB
    first_half = iota((ROWS, LANE), 1) < LANE // 2
    last = kv_part[:, cols.start - edge :]
    last = jnp.where((row & 7) == sub, jnp.where(first_half, high, middle), last)
    last = jnp.where((row & 7) == sub + 1, jnp.where(first_half, low, 0.0), last)
    message[:, edge + LANE : cols.start] = kv_part[:, LANE : cols.start - edge].astype(BF16)
    message[:, cols] = last.astype(BF16)
    kv_copy = pltpu.make_async_copy(message.at[:, edge:], out_hbm.at[:, edge:], sems.at[2])
    kv_copy.start()
    carried_copy.wait()
    q_copy.wait()
    kv_copy.wait()


def late_out_kernel(carried_ref, table_ref, out_ref):
    peer_rows = (iota((ROWS, LANE), 0) & 7) < SPLIT_SUB
    q_matrix, kv_matrix = to_peers(table_ref[0, LATE]), to_peers(table_ref[1, LATE])
    out_ref[...] = by_kind(q_matrix, kv_matrix, carried_ref[...], peer_rows).astype(BF16)


def halves(x):
    high = x.astype(BF16)
    return high, (x - high.astype(F32)).astype(BF16)


def product(a, b, op):
    return op(a[0], b[0]) + (op(a[0], b[1]) + op(a[1], b[0]))


def newton_step(x_ref):
    x = x_ref[...]
    parts = halves(x)
    square = product(parts, parts, dot_nt)
    square_parts = halves(square)
    polynomial = NEWTON_SECOND * square + NEWTON_THIRD * product(square_parts, square_parts, dot)
    x_ref[...] = NEWTON_FIRST * x + product(halves(polynomial), parts, dot)


def owner_kernel(
    node_ref, in_ref, q_mom, kv_mom, fill_ref, out_ref, q_new, kv_new, q_x, kv_x, q_half, kv_half, tiles_ref
):
    node = node_ref[0]
    received = dot(unpack_matrix(), in_ref[...])
    arrived = from_tiles(received.astype(BF16), q_half, kv_half)
    for kind, gradient, mom, new, x_ref in (
        (0, arrived[0], q_mom, q_new, q_x),
        (1, arrived[1], kv_mom, kv_new, kv_x),
    ):
        used = fill_ref[kind, pl.ds(node, 1), :1] > 0.5
        carried = MOMENTUM_RATE * mom[0, 0, 0].astype(F32) + gradient
        new[0, 0, 0] = jnp.where(used, carried, 0.0).astype(BF16)
        direction = jnp.where(used, gradient + MOMENTUM_RATE * carried, gradient)
        norm = jnp.sqrt(jnp.sum(direction * direction)) + EPSILON
        x_ref[...] = direction / norm

    def body(_, carry):
        newton_step(q_x)
        newton_step(kv_x)
        return carry

    lax.fori_loop(0, STEPS, body, 0)
    outgoing = to_message((q_x[...] * Q_SCALE).astype(BF16), (kv_x[...] * KV_SCALE).astype(BF16), tiles_ref)
    out_ref[...] = outgoing.astype(BF16)


def owner_step(node, arrived, momentum_query, momentum_kv, fill):
    q_slot = pl.BlockSpec((1, 1, 1, Q_ROWS, Q_COLS), lambda i: (0, 0, 0, 0, 0))
    kv_slot = pl.BlockSpec((1, 1, 1, KV_ROWS, KV_COLS), lambda i: (0, 0, 0, 0, 0))
    return call(
        owner_kernel,
        (
            pltpu.HBM((ROWS, MSG), BF16),
            pltpu.HBM((1, 1, 2, Q_ROWS, Q_COLS), BF16),
            pltpu.HBM((1, 1, 2, KV_ROWS, KV_COLS), BF16),
        ),
        node,
        arrived,
        in_hbm(momentum_query),
        in_hbm(momentum_kv),
        fill,
        grid=(1,),
        in_specs=[pl.BlockSpec(memory_space=pltpu.SMEM), whole(ROWS, MSG), q_slot, kv_slot, whole(2, NODES, LANE)],
        out_specs=[whole(ROWS, MSG), q_slot, kv_slot],
        scratch_shapes=[
            pltpu.VMEM((Q_ROWS, Q_COLS), F32),
            pltpu.VMEM((KV_ROWS, KV_COLS), F32),
            pltpu.VMEM((Q_ROWS, Q_COLS), BF16),
            pltpu.VMEM((KV_ROWS, KV_COLS), BF16),
            pltpu.VMEM((ROWS, MSG), BF16),
        ],
    )


def settle_kernel(in_ref, arrived_ref, q_old, kv_old, q_new, kv_new, factor_ref, q_half, kv_half):
    matrix = unpack_matrix()
    late = dot(matrix, in_ref[...]).astype(BF16)
    q_late, kv_late = from_tiles(late, q_half, kv_half)
    q_new[0, 0, 0] = q_late.astype(BF16)
    kv_new[0, 0, 0] = kv_late.astype(BF16)

    rows, cols = place(PEAK_TILE)
    parts = dot(matrix, arrived_ref[:, cols])
    top, bottom = parts[rows], parts[place(PEAK_TILE + 1)[0]]
    peaks = jnp.max((top[:, :BLOCKS] + top[:, BLOCKS:]) + bottom[:, :BLOCKS], axis=0, keepdims=True)
    diagonal = iota((BLOCKS, BLOCKS), 0) == iota((BLOCKS, BLOCKS), 1)
    peak_col = jnp.sum(jnp.where(diagonal, jnp.broadcast_to(peaks, (BLOCKS, BLOCKS)), 0.0), axis=1, keepdims=True)
    shrink = jnp.minimum(1.0, CLIP_LEVEL / peak_col)
    factor_ref[0] = jnp.broadcast_to(jnp.sqrt(shrink), (BLOCKS, LANE))
    factor_ref[1] = jnp.broadcast_to(shrink, (BLOCKS, LANE))


def settle(late, arrived, q_momentum, kv_momentum):
    anywhere = pl.BlockSpec(memory_space=pl.ANY)
    return call(
        settle_kernel,
        (
            shape((1, 1, 2, Q_ROWS, Q_COLS), BF16),
            shape((1, 1, 2, KV_ROWS, KV_COLS), BF16),
            shape((2, BLOCKS, LANE), F32),
        ),
        late,
        arrived,
        q_momentum,
        kv_momentum,
        grid=(1,),
        in_specs=[whole(ROWS, MSG), whole(ROWS, MSG), anywhere, anywhere],
        out_specs=[
            pl.BlockSpec((1, 1, 1, Q_ROWS, Q_COLS), lambda i: (0, 0, 1, 0, 0)),
            pl.BlockSpec((1, 1, 1, KV_ROWS, KV_COLS), lambda i: (0, 0, 1, 0, 0)),
            whole(2, BLOCKS, LANE),
        ],
        scratch_shapes=[pltpu.VMEM((Q_ROWS, Q_COLS), BF16), pltpu.VMEM((KV_ROWS, KV_COLS), BF16)],
        input_output_aliases={2: 0, 3: 1},
    )


def finish_kernel(
    node_ref, in_ref, table_ref, factor_ref, weight_hbm, update_hbm, weight_new_hbm, kv_update_ref,
    weight, update, sems,
):
    fetch = pltpu.make_async_copy(weight_hbm, weight, sems.at[0])
    fetch.start()
    edge = SPLIT * LANE
    kv_rows = dot(to_tiles(table_ref[1, SEND_BACK]), in_ref[:, edge:])
    for r, ct, tile in tiles_of("kv"):
        rows, cols = place(tile)
        lanes = slice(cols.start - edge, cols.stop - edge)
        kv_update_ref[r, :, ct * LANE : (ct + 1) * LANE] = kv_rows[rows, lanes].astype(BF16)
    q_rows = dot(to_tiles(table_ref[0, SEND_BACK]), in_ref[:, : edge + LANE])
    fetch.wait()
    copies = []
    for r in range(Q_OWN):
        factor = jnp.where(node_ref[0] * Q_OWN + r < QN, factor_ref[0], factor_ref[1])
        factor = factor.reshape(LAYERS, PER_GROUP, LANE)
        for ct in range(Q_TILES):
            rows, cols = place(r * Q_TILES + ct)
            lanes = slice(ct * LANE, (ct + 1) * LANE)
            step = q_rows[rows, cols].reshape(LAYERS, PER_GROUP, LANE)
            update[:, r, :, lanes] = step.astype(BF16)
            old = weight[:, r, :, lanes]
            weight[:, r, :, lanes] = (old - LEARN_RATE * (step + DECAY_RATE * old)) * factor
        copies.append(pltpu.make_async_copy(update.at[:, r], update_hbm.at[:, r], sems.at[1 + 2 * r]))
        copies.append(pltpu.make_async_copy(weight.at[:, r], weight_new_hbm.at[:, r], sems.at[2 + 2 * r]))
        copies[-2].start()
        copies[-1].start()
    for copy in copies:
        copy.wait()


def finish(node, returned, table, factors, weight_query):
    q_dims = (LAYERS, Q_OWN, PER_GROUP, Q_COLS)
    kv_dims = (KV_OWN, BLOCKS, KV_COLS)
    outside = pl.BlockSpec(memory_space=pltpu.HBM)
    return call(
        finish_kernel,
        (pltpu.HBM(q_dims, BF16), pltpu.HBM(q_dims, F32), shape(kv_dims, BF16)),
        node,
        returned,
        table,
        factors,
        in_hbm(weight_query),
        grid=(1,),
        in_specs=[
            pl.BlockSpec(memory_space=pltpu.SMEM),
            whole(ROWS, MSG),
            whole(2, 4, NODES, BLOCKS),
            whole(2, BLOCKS, LANE),
            outside,
        ],
        out_specs=[outside, outside, whole(*kv_dims)],
        scratch_shapes=[
            pltpu.VMEM(q_dims, F32),
            pltpu.VMEM(q_dims, BF16),
            pltpu.SemaphoreType.DMA((1 + 2 * Q_OWN,)),
        ],
    )


def exchange(message):
    return lax.all_to_all(message, "fsdp", split_axis=0, concat_axis=0, tiled=True)


def on_device(
    grad_query, grad_kv, momentum_query, momentum_kv, weight_query, weight_kv, owner_query, owner_kv, max_logits
):
    my_group = lax.axis_index("dp")
    my_node = lax.axis_index("fsdp")

    node = my_node.astype(I32).reshape(1)
    forward = [(i, (i + 1) % GROUPS) for i in range(GROUPS)]
    backward = [(i, (i + 3) % GROUPS) for i in range(GROUPS)]

    def turn(*steps):
        return (my_group.astype(I32) + jnp.asarray(steps, I32)) % GROUPS

    q_grads = jnp.transpose(grad_query[0], (0, 2, 1, 3))
    kv_grads = jnp.transpose(grad_kv[0], (0, 2, 1, 3))
    peaks = max_logits[0]
    ring_shape = (shape((RING, MSG), BF16),) * 2
    to_next, to_last = arrange_call(first_kernel, turn(2, 1, 3), q_grads, kv_grads, peaks, (), ring_shape)
    to_next, to_last, momentum_query, momentum_kv = lax.optimization_barrier(
        (to_next, to_last, momentum_query, momentum_kv)
    )
    from_last = lax.ppermute(to_next, "dp", forward)
    from_next = lax.ppermute(to_last, "dp", backward)
    late_in = exchange(late_message(momentum_query, momentum_kv))
    table, over, fill = tables(turn(0), owner_query, owner_kv)
    hint = pl.CostEstimate(flops=10**12, bytes_accessed=10**10, transcendentals=0)
    to_next, to_last = arrange_call(
        combine_kernel, turn(1, 3), q_grads, kv_grads, peaks, (from_last, from_next),
        ring_shape, hint,
    )
    sum_last = lax.ppermute(to_next, "dp", forward)
    sum_next = lax.ppermute(to_last, "dp", backward)
    (mine,) = arrange_call(mine_kernel, turn(0), q_grads, kv_grads, peaks, (), (pltpu.HBM((ROWS, MSG), BF16),))
    earlier = call(earlier_kernel, shape((ROWS, MSG), BF16), late_in, table)

    outside = pl.BlockSpec(memory_space=pltpu.HBM)
    message, carried = call(
        send_kernel,
        (pltpu.HBM((ROWS, MSG), BF16), pltpu.HBM((ROWS, MSG), BF16)),
        mine, sum_last, sum_next, from_last, from_next, earlier, table, over,
        grid=(1,),
        in_specs=[whole(ROWS, MSG)] + [whole(RING, MSG)] * 4 + [whole(ROWS, MSG)]
        + [whole(2, 4, NODES, BLOCKS), whole(2, BLOCKS, LANE)],
        out_specs=[outside, outside],
        scratch_shapes=[pltpu.VMEM((ROWS, MSG), BF16)] * 3 + [pltpu.SemaphoreType.DMA((3,))],
    )
    late_out = call(late_out_kernel, pltpu.HBM((ROWS, MSG), BF16), carried, table)
    arrived, late_out = lax.optimization_barrier((exchange(message), late_out))
    late = exchange(late_out)
    outgoing, q_momentum, kv_momentum = owner_step(node, arrived, momentum_query, momentum_kv, fill)
    late, outgoing = lax.optimization_barrier((late, outgoing))
    returned = exchange(outgoing)
    q_momentum, kv_momentum, factors = settle(late, arrived, q_momentum, kv_momentum)
    q_update, q_weight, kv_update = finish(
        node, returned, table, factors, jnp.transpose(weight_query, (0, 2, 1, 3))
    )
    kv_update = jnp.transpose(kv_update.reshape(KV_OWN, LAYERS, PER_GROUP, KV_COLS), (1, 2, 0, 3))
    kv_index = my_node * KV_OWN + jnp.arange(KV_OWN, dtype=I32)
    root_shrink = factors[0, :, 0].reshape(LAYERS, PER_GROUP)
    kv_factor = jnp.where(kv_index[None, None, :, None] < KN, root_shrink[:, :, None, None], 1.0)
    kv_weight = (weight_kv - LEARN_RATE * (kv_update.astype(F32) + DECAY_RATE * weight_kv)) * kv_factor
    return (
        jnp.transpose(q_update, (0, 2, 1, 3)),
        kv_update,
        jnp.transpose(q_weight, (0, 2, 1, 3)),
        kv_weight,
        q_momentum,
        kv_momentum,
    )


def solution(mesh):
    return jax.shard_map(
        on_device,
        mesh=mesh,
        in_specs=(
            P("dp", None, None, "fsdp", None),
            P("dp", None, None, "fsdp", None),
            P("dp", "fsdp", None, None, None),
            P("dp", "fsdp", None, None, None),
            P(None, "dp", "fsdp", None),
            P(None, "dp", "fsdp", None),
            P(),
            P(),
            P(("dp", "fsdp"), None, None),
        ),
        out_specs=(
            P(None, "dp", "fsdp", None),
            P(None, "dp", "fsdp", None),
            P(None, "dp", "fsdp", None),
            P(None, "dp", "fsdp", None),
            P("dp", "fsdp", None, None, None),
            P("dp", "fsdp", None, None, None),
        ),
        check_vma=False,
    )
```

```python
import math

import jax
import jax.numpy as jnp
from jax import lax
from jax.experimental import pallas as pl
from jax.experimental.pallas import tpu as pltpu
from jax.sharding import PartitionSpec as P

QN = 128
KN = 128
STEPS = 5
LAYERS = 4
HEADS = 64
GROUPS = 4
PER_GROUP = 16
NODES = 64
BLOCKS = 64
Q_ROWS, Q_COLS = 192, 1536
KV_ROWS, KV_COLS = 256, 512
Q_OWN, KV_OWN = Q_ROWS // NODES, KV_ROWS // NODES
LANE = 128
Q_TILES, KV_TILES = Q_COLS // LANE, KV_COLS // LANE
SUB = 8
MSG_COLS = 7
MSG = MSG_COLS * LANE
ROWS = NODES * SUB
HALF = ROWS // 2
EXTRA = ROWS // 4
RING = ROWS - EXTRA
PEAK_TILE = Q_OWN * Q_TILES + KV_OWN * KV_TILES
LATE_MSG = MSG - LANE
REST = KV_TILES
SPLIT = Q_OWN * Q_TILES // SUB
SPLIT_SUB = Q_OWN * Q_TILES % SUB

MOMENTUM_RATE = 0.95
LEARN_RATE = 0.02
DECAY_RATE = 0.1
CLIP_LEVEL = 100.0
NEWTON_FIRST = 3.4445
NEWTON_SECOND = -4.775
NEWTON_THIRD = 2.0315
EPSILON = 1e-07
Q_SCALE = 0.2 * math.sqrt(max(Q_ROWS, Q_COLS))
KV_SCALE = 0.2 * math.sqrt(max(KV_ROWS, KV_COLS))

F32 = jnp.float32
BF16 = jnp.bfloat16
I32 = jnp.int32
PARAMS = pltpu.CompilerParams(vmem_limit_bytes=24 * 1024 * 1024)


def place(tile):
    col, sub = divmod(tile, SUB)
    return slice(sub * BLOCKS, (sub + 1) * BLOCKS), slice(col * LANE, (col + 1) * LANE)


def tiles_of(kind):
    if kind == "q":
        return [(r, ct, r * Q_TILES + ct) for r in range(Q_OWN) for ct in range(Q_TILES)]
    base = Q_OWN * Q_TILES
    return [(r, ct, base + r * KV_TILES + ct) for r in range(KV_OWN) for ct in range(KV_TILES)]


def in_hbm(x):
    return pltpu.with_memory_space_constraint(x, pltpu.HBM)


def iota(shape, dim):
    return lax.broadcasted_iota(I32, shape, dim)


def dot(a, b):
    return jnp.dot(a, b, preferred_element_type=F32)


def dot_nt(a, b):
    return lax.dot_general(a, b, (((1,), (1,)), ((), ())), preferred_element_type=F32)


def one(cond):
    return jnp.where(cond, 1.0, 0.0).astype(BF16)


def pack_matrix():
    row, col = iota((ROWS, ROWS), 0), iota((ROWS, ROWS), 1)
    return one(((row >> 3) == (col & 63)) & ((row & 7) == (col >> 6)))


def unpack_matrix():
    row, col = iota((ROWS, ROWS), 0), iota((ROWS, ROWS), 1)
    return one(((row & 63) == (col >> 3)) & ((row >> 6) == (col & 7)))


def natural_matrix(own):
    size = own * NODES
    row, col = iota((size, size), 0), iota((size, size), 1)
    return one(row == (col & 63) * own + (col >> 6))


def split_matrix(own):
    size = own * NODES
    row, col = iota((size, size), 0), iota((size, size), 1)
    return one(col == (row & 63) * own + (row >> 6))


def to_message(q_natural, kv_natural, tiles_ref):
    q_split = dot(split_matrix(Q_OWN), q_natural).astype(BF16)
    kv_split = dot(split_matrix(KV_OWN), kv_natural).astype(BF16)
    tiles_ref[:, SPLIT * LANE :] = jnp.zeros((ROWS, MSG - SPLIT * LANE), BF16)
    for r, ct, tile in tiles_of("q"):
        rows, cols = place(tile)
        tiles_ref[rows, cols] = q_split[r * NODES : (r + 1) * NODES, ct * LANE : (ct + 1) * LANE]
    for r, ct, tile in tiles_of("kv"):
        rows, cols = place(tile)
        tiles_ref[rows, cols] = kv_split[r * NODES : (r + 1) * NODES, ct * LANE : (ct + 1) * LANE]
    return dot(pack_matrix(), tiles_ref[...])


def from_tiles(tiles, q_ref, kv_ref):
    for r, ct, tile in tiles_of("q"):
        rows, cols = place(tile)
        q_ref[r * NODES : (r + 1) * NODES, ct * LANE : (ct + 1) * LANE] = tiles[rows, cols]
    for r, ct, tile in tiles_of("kv"):
        rows, cols = place(tile)
        kv_ref[r * NODES : (r + 1) * NODES, ct * LANE : (ct + 1) * LANE] = tiles[rows, cols]
    return dot(natural_matrix(Q_OWN), q_ref[...]), dot(natural_matrix(KV_OWN), kv_ref[...])


def by_kind(q_matrix, kv_matrix, source, q_rows):
    edge = SPLIT * LANE
    q_part = dot(q_matrix, source[:, : edge + LANE])
    kv_part = dot(kv_matrix, source[:, edge:])
    mixed = jnp.where(q_rows, q_part[:, edge:], kv_part[:, :LANE])
    return jnp.concatenate([q_part[:, :edge], mixed, kv_part[:, LANE:]], axis=1)


def call(kernel, out_shape, *operands, **options):
    return pl.pallas_call(kernel, out_shape=out_shape, compiler_params=PARAMS, **options)(*operands)


def whole(*dims):
    return pl.BlockSpec(dims, lambda i: (0,) * len(dims))


HERE = pl.BlockSpec(memory_space=pltpu.VMEM)


def shape(dims, dtype):
    return jax.ShapeDtypeStruct(dims, dtype)


def parts_of(value):
    high = value.astype(BF16).astype(F32)
    middle = (value - high).astype(BF16).astype(F32)
    return high, middle, (value - high) - middle


def peak_tile(column):
    high, middle, low = parts_of(column)
    lane = iota((column.shape[0], LANE), 1)
    return jnp.where(lane == 0, high, jnp.where(lane == 1, middle, jnp.where(lane == 2, low, 0.0))).astype(BF16)


def peak_column(tile):
    lane = iota(tile.shape, 1)
    return jnp.sum(jnp.where(lane < 3, tile.astype(F32), 0.0), axis=1, keepdims=True)


def group_tiles(group, q_ref, kv_ref, peak_ref, put):
    for tile in range(PEAK_TILE + 1, MSG_COLS * SUB):
        rows, cols = place(tile)
        put(rows.start, cols, jnp.zeros((BLOCKS, LANE), BF16))
    rows, cols = place(PEAK_TILE)
    for layer in range(LAYERS):
        spread = jnp.broadcast_to(peak_ref[layer : layer + 1, :], (PER_GROUP, HEADS))
        mine = iota((PER_GROUP, HEADS), 1) == iota((PER_GROUP, HEADS), 0) + group * PER_GROUP
        column = jnp.sum(jnp.where(mine, spread, 0.0), axis=1, keepdims=True)
        put(rows.start + layer * PER_GROUP, cols, peak_tile(column))
    for kind, ref in (("q", q_ref), ("kv", kv_ref)):
        for r, ct, tile in tiles_of(kind):
            rows, cols = place(tile)
            for layer in range(LAYERS):
                put(rows.start + layer * PER_GROUP, cols, ref[layer, r, :, ct * LANE : (ct + 1) * LANE])


def window(start, size):
    return slice(start, start + size)


def first_kernel(
    group_ref, q_far, kv_far, q_next, kv_next, q_last, kv_last, peak_ref, forward_out, backward_out
):
    def put_far(start, cols, value):
        out = (forward_out, backward_out)[start // HALF]
        out[window(start % HALF, value.shape[0]), cols] = value

    def put_next(start, cols, value):
        if start >= ROWS - EXTRA:
            forward_out[window(start - ROWS + EXTRA + HALF, value.shape[0]), cols] = value

    def put_last(start, cols, value):
        if start < EXTRA:
            backward_out[window(start + HALF, value.shape[0]), cols] = value

    group_tiles(group_ref[0], q_far, kv_far, peak_ref, put_far)
    group_tiles(group_ref[1], q_next, kv_next, peak_ref, put_next)
    group_tiles(group_ref[2], q_last, kv_last, peak_ref, put_last)


def mine_kernel(group_ref, q_ref, kv_ref, peak_ref, out_ref):
    def put(start, cols, value):
        out_ref[window(start, value.shape[0]), cols] = value

    group_tiles(group_ref[0], q_ref, kv_ref, peak_ref, put)


def combine_kernel(
    group_ref, q_next, kv_next, q_last, kv_last, peak_ref, from_last, from_next, next_out, last_out
):
    def put_next(start, cols, value):
        if start >= ROWS - EXTRA:
            return
        if start < HALF:
            value = (value.astype(F32) + from_last[window(start, value.shape[0]), cols].astype(F32)).astype(BF16)
        next_out[window(start, value.shape[0]), cols] = value

    def put_last(start, cols, value):
        if start < EXTRA:
            return
        here = window(start - EXTRA, value.shape[0])
        if start >= HALF:
            far = from_next[window(start - HALF, value.shape[0]), cols]
            if window(start // BLOCKS * BLOCKS, BLOCKS) == peak_rows and cols == peak_cols:
                value = peak_tile(jnp.maximum(peak_column(value), peak_column(far)))
            else:
                value = (value.astype(F32) + far.astype(F32)).astype(BF16)
        last_out[here, cols] = value

    peak_rows, peak_cols = place(PEAK_TILE)
    group_tiles(group_ref[0], q_next, kv_next, peak_ref, put_next)
    group_tiles(group_ref[1], q_last, kv_last, peak_ref, put_last)


def arrange_call(kernel, groups, grad_query, grad_kv, peaks, extra, out_shape, hint=None):
    count = groups.shape[0]

    def at(index):
        return [
            pl.BlockSpec((LAYERS, Q_OWN, PER_GROUP, Q_COLS), lambda i, g: (0, 0, g[index], 0)),
            pl.BlockSpec((LAYERS, KV_OWN, PER_GROUP, KV_COLS), lambda i, g: (0, 0, g[index], 0)),
        ]

    def all_of(x):
        return pl.BlockSpec(x.shape, lambda i, g: (0,) * len(x.shape))

    return pl.pallas_call(
        kernel,
        out_shape=out_shape,
        grid_spec=pltpu.PrefetchScalarGridSpec(
            num_scalar_prefetch=1,
            grid=(1,),
            in_specs=sum([at(index) for index in range(count)], []) + [all_of(peaks)] + [HERE] * len(extra),
            out_specs=[all_of(x) if hint is None and count == 1 else HERE for x in out_shape],
        ),
        compiler_params=PARAMS,
        cost_estimate=hint,
    )(groups, *([in_hbm(grad_query), grad_kv] * count), peaks, *extra)


SEND, LATE, SEND_BACK, LATE_BACK = range(4)


def table_kernel(group_ref, q_ref, kv_ref, table_ref, over_ref, fill_ref):
    group = group_ref[0]
    down, across = iota((NODES, BLOCKS), 0), iota((NODES, BLOCKS), 1)

    def count(cond, axis):
        return jnp.sum(jnp.where(cond, 1.0, 0.0), axis=axis, keepdims=True)

    for kind, ref in enumerate((q_ref, kv_ref)):
        owner_row = jnp.zeros((SUB, BLOCKS), F32)
        for layer in range(LAYERS):
            piece = jnp.broadcast_to(ref[group, layer].astype(F32), (SUB, PER_GROUP)).astype(BF16)
            spot = iota((PER_GROUP, BLOCKS), 1) == iota((PER_GROUP, BLOCKS), 0) + layer * PER_GROUP
            owner_row += dot(piece, one(spot))
        owner_row = owner_row[:1].astype(I32)
        spread = jnp.broadcast_to(owner_row, (BLOCKS, BLOCKS))
        owner_col = jnp.sum(jnp.where(down == across, spread, 0).astype(F32), axis=1, keepdims=True).astype(I32)
        same = owner_col == owner_row
        slot_col = count(same & (across < down), 1)
        slot_row = count(same & (down < across), 0)
        hits = down == owner_row
        hits_back = owner_col == across
        fill_col, fill_row = count(hits, 1), count(hits_back, 0)
        over_col, over_row = slot_col > 0.5, slot_row > 0.5
        free_col, free_row = fill_col < 0.5, fill_row < 0.5
        over_rank_col, over_rank_row = count(over_row & (across < down), 1), count(over_col & (down < across), 0)
        free_rank_col, free_rank_row = count(free_row & (across < down), 1), count(free_col & (down < across), 0)
        table_ref[kind, SEND] = one(
            (hits & ~over_row) | (free_col & over_row & (free_rank_col == over_rank_row))
        )
        table_ref[kind, LATE] = one(hits & over_row)
        table_ref[kind, SEND_BACK] = one(
            (hits_back & ~over_col) | (free_row & over_col & (free_rank_row == over_rank_col))
        )
        table_ref[kind, LATE_BACK] = one(hits_back & over_col)
        over_ref[kind] = jnp.broadcast_to(jnp.where(over_col, 1.0, 0.0), (BLOCKS, LANE))
        fill_ref[kind] = jnp.broadcast_to(fill_col, (BLOCKS, LANE))


def tables(group, owner_query, owner_kv):
    return call(
        table_kernel,
        (shape((2, 4, NODES, BLOCKS), BF16), shape((2, BLOCKS, LANE), F32), shape((2, NODES, LANE), F32)),
        group,
        jnp.transpose(owner_query, (0, 1, 3, 2)),
        jnp.transpose(owner_kv, (0, 1, 3, 2)),
        in_specs=[pl.BlockSpec(memory_space=pltpu.SMEM)] + [pl.BlockSpec(memory_space=pltpu.VMEM)] * 2,
    )


def to_peers(table):
    rows = one((iota((ROWS, NODES), 0) >> 3) == iota((ROWS, NODES), 1))
    cols = one(iota((BLOCKS, ROWS), 0) == (iota((BLOCKS, ROWS), 1) & 63))
    wide = dot(dot(rows, table).astype(BF16), cols)
    row, col = iota((ROWS, ROWS), 0), iota((ROWS, ROWS), 1)
    return jnp.where((row & 7) == (col >> 6), wide, 0.0).astype(BF16)


def to_tiles(table):
    rows = one((iota((ROWS, BLOCKS), 0) & 63) == iota((ROWS, BLOCKS), 1))
    cols = one(iota((NODES, ROWS), 0) == (iota((NODES, ROWS), 1) >> 3))
    wide = dot(dot(rows, table).astype(BF16), cols)
    row, col = iota((ROWS, ROWS), 0), iota((ROWS, ROWS), 1)
    return jnp.where((row >> 6) == (col & 7), wide, 0.0).astype(BF16)


def expand_kernel(table_ref, send_ref, late_back_ref, back_ref):
    for kind in range(2):
        send_ref[kind] = to_peers(table_ref[kind, SEND])
        late_back_ref[kind] = to_tiles(table_ref[kind, LATE_BACK])
        back_ref[kind] = to_tiles(table_ref[kind, SEND_BACK])


def expand(table):
    return call(expand_kernel, (pltpu.HBM((2, ROWS, ROWS), BF16),) * 3, table)


def late_kernel(q_ref, kv_ref, out_ref, tiles_ref):
    out_ref[...] = to_message(q_ref[0, 0, 0], kv_ref[0, 0, 0], tiles_ref).astype(BF16)


def late_message(momentum_query, momentum_kv):
    return call(
        late_kernel,
        pltpu.HBM((ROWS, MSG), BF16),
        in_hbm(momentum_query),
        in_hbm(momentum_kv),
        grid=(1,),
        in_specs=[
            pl.BlockSpec((1, 1, 1, Q_ROWS, Q_COLS), lambda i: (0, 0, 1, 0, 0)),
            pl.BlockSpec((1, 1, 1, KV_ROWS, KV_COLS), lambda i: (0, 0, 1, 0, 0)),
        ],
        out_specs=pl.BlockSpec((ROWS, MSG), lambda i: (0, 0)),
        scratch_shapes=[pltpu.VMEM((ROWS, MSG), BF16)],
    )


def earlier_kernel(late_in_ref, matrix_ref, out_ref):
    tile_rows = iota((ROWS, LANE), 0) < SPLIT_SUB * BLOCKS
    out_ref[...] = by_kind(matrix_ref[0], matrix_ref[1], late_in_ref[...], tile_rows).astype(BF16)


def send_kernel(
    mine_ref, last_ref, next_ref, first_last, first_next, earlier_ref, matrix_ref, over_ref, out_hbm, carried_hbm,
    chosen, carried, message, sems,
):
    row = iota((ROWS, LANE), 0)
    q_over = jnp.concatenate([over_ref[0]] * SUB, axis=0)
    kv_over = jnp.concatenate([over_ref[1]] * SUB, axis=0)
    for col in range(MSG_COLS):
        lanes = slice(col * LANE, (col + 1) * LANE)
        last = jnp.concatenate([last_ref[:, lanes], first_last[:, lanes]], axis=0).astype(F32)
        following = jnp.concatenate([first_next[:, lanes], next_ref[:, lanes]], axis=0).astype(F32)
        reduced = mine_ref[:, lanes].astype(F32) + (last + following)
        reduced = reduced.astype(BF16).astype(F32)
        moved = MOMENTUM_RATE * earlier_ref[:, lanes].astype(F32) + reduced
        carried[:, lanes] = moved.astype(BF16)
        if col < SPLIT:
            mask = q_over
        elif col == SPLIT:
            mask = jnp.where(row < SPLIT_SUB * BLOCKS, q_over, kv_over)
        else:
            mask = kv_over
        chosen[:, lanes] = jnp.where(mask > 0.5, reduced + MOMENTUM_RATE * moved, reduced).astype(BF16)
    carried_copy = pltpu.make_async_copy(carried, carried_hbm, sems.at[0])
    carried_copy.start()
    edge = SPLIT * LANE
    q_part = dot(matrix_ref[0], chosen[:, : edge + LANE])
    message[:, :edge] = q_part[:, :edge].astype(BF16)
    q_copy = pltpu.make_async_copy(message.at[:, :edge], out_hbm.at[:, :edge], sems.at[1])
    q_copy.start()
    kv_part = dot(matrix_ref[1], chosen[:, edge:])
    peer_rows = (row & 7) < SPLIT_SUB
    message[:, edge : edge + LANE] = jnp.where(peer_rows, q_part[:, edge:], kv_part[:, :LANE]).astype(BF16)
    rows, cols = place(PEAK_TILE)
    peak = jnp.maximum(peak_column(mine_ref[rows, cols]), peak_column(last_ref[rows, cols]))
    peak = jnp.maximum(peak, peak_column(next_ref[rows.start - EXTRA : rows.stop - EXTRA, cols]))
    spot = iota((BLOCKS, LANE), 0) == (iota((BLOCKS, LANE), 1) & 63)
    peak = jnp.sum(jnp.where(spot, jnp.broadcast_to(peak, (BLOCKS, LANE)), 0.0), axis=0, keepdims=True)
    high, middle, low = parts_of(peak)
    sub = PEAK_TILE % SUB
    first_half = iota((ROWS, LANE), 1) < LANE // 2
    last = kv_part[:, cols.start - edge :]
    last = jnp.where((row & 7) == sub, jnp.where(first_half, high, middle), last)
    last = jnp.where((row & 7) == sub + 1, jnp.where(first_half, low, 0.0), last)
    message[:, edge + LANE : cols.start] = kv_part[:, LANE : cols.start - edge].astype(BF16)
    message[:, cols] = last.astype(BF16)
    kv_copy = pltpu.make_async_copy(message.at[:, edge:], out_hbm.at[:, edge:], sems.at[2])
    kv_copy.start()
    carried_copy.wait()
    q_copy.wait()
    kv_copy.wait()


def late_out_kernel(carried_ref, table_ref, out_ref, rest_ref):
    row = iota((ROWS, LANE), 0)
    q_matrix, kv_matrix = to_peers(table_ref[0, LATE]), to_peers(table_ref[1, LATE])
    placed = by_kind(q_matrix, kv_matrix, carried_ref[...], (row & 7) < SPLIT_SUB)
    out_ref[...] = placed[:, :LATE_MSG].astype(BF16)
    moved = pltpu.roll(placed[:, LATE_MSG:], REST, 0)
    rest_ref[...] = jnp.where((row & 7) >= REST, moved, 0.0).astype(BF16)


def halves(x):
    high = x.astype(BF16)
    return high, (x - high.astype(F32)).astype(BF16)


def product(a, b, op):
    size = a[0].shape[0]
    both = op(jnp.concatenate(a, axis=0), b[0])
    return both[:size] + (both[size:] + op(a[0], b[1]))


def newton_step(refs):
    values = [ref[...] for ref in refs]
    parts = [halves(x) for x in values]
    squares = [product(h, h, dot_nt) for h in parts]
    square_parts = [halves(square) for square in squares]
    polynomials = [
        NEWTON_SECOND * square + NEWTON_THIRD * product(h, h, dot) for square, h in zip(squares, square_parts)
    ]
    for ref, x, h, polynomial in zip(refs, values, parts, polynomials):
        ref[...] = NEWTON_FIRST * x + product(halves(polynomial), h, dot)


def owner_kernel(
    node_ref, in_ref, q_mom, kv_mom, fill_ref, rest_ref, out_ref, q_new, kv_new, q_x, kv_x, q_half, kv_half, tiles_ref
):
    node = node_ref[0]
    received = dot(unpack_matrix(), in_ref[...])
    arrived = from_tiles(received.astype(BF16), q_half, kv_half)
    for kind, gradient, mom, new, x_ref in (
        (0, arrived[0], q_mom, q_new, q_x),
        (1, arrived[1], kv_mom, kv_new, kv_x),
    ):
        used = fill_ref[kind, pl.ds(node, 1), :1] > 0.5
        carried = MOMENTUM_RATE * mom[0, 0, 0].astype(F32) + gradient
        new[0, 0, 0] = jnp.where(used, carried, 0.0).astype(BF16)
        direction = jnp.where(used, gradient + MOMENTUM_RATE * carried, gradient)
        norm = jnp.sqrt(jnp.sum(direction * direction)) + EPSILON
        x_ref[...] = direction / norm

    def body(_, carry):
        newton_step((q_x, kv_x))
        return carry

    lax.fori_loop(0, STEPS, body, 0)
    outgoing = to_message((q_x[...] * Q_SCALE).astype(BF16), (kv_x[...] * KV_SCALE).astype(BF16), tiles_ref)
    out_ref[:, :LATE_MSG] = outgoing[:, :LATE_MSG].astype(BF16)
    out_ref[:, LATE_MSG:] = (outgoing[:, LATE_MSG:] + rest_ref[...].astype(F32)).astype(BF16)


def owner_step(node, arrived, momentum_query, momentum_kv, fill, rest):
    q_slot = pl.BlockSpec((1, 1, 1, Q_ROWS, Q_COLS), lambda i: (0, 0, 0, 0, 0))
    kv_slot = pl.BlockSpec((1, 1, 1, KV_ROWS, KV_COLS), lambda i: (0, 0, 0, 0, 0))
    return call(
        owner_kernel,
        (
            pltpu.HBM((ROWS, MSG), BF16),
            pltpu.HBM((1, 1, 2, Q_ROWS, Q_COLS), BF16),
            pltpu.HBM((1, 1, 2, KV_ROWS, KV_COLS), BF16),
        ),
        node,
        arrived,
        in_hbm(momentum_query),
        in_hbm(momentum_kv),
        fill,
        in_hbm(rest),
        grid=(1,),
        in_specs=[pl.BlockSpec(memory_space=pltpu.SMEM), HERE, q_slot, kv_slot, whole(2, NODES, LANE), whole(ROWS, LANE)],
        out_specs=[whole(ROWS, MSG), q_slot, kv_slot],
        scratch_shapes=[
            pltpu.VMEM((Q_ROWS, Q_COLS), F32),
            pltpu.VMEM((KV_ROWS, KV_COLS), F32),
            pltpu.VMEM((Q_ROWS, Q_COLS), BF16),
            pltpu.VMEM((KV_ROWS, KV_COLS), BF16),
            pltpu.VMEM((ROWS, MSG), BF16),
        ],
    )


def settle_kernel(in_ref, arrived_ref, q_old, q_new, kv_part, factor_ref, q_half, kv_half):
    matrix = unpack_matrix()
    late = dot(matrix, in_ref[...]).astype(BF16)
    for kind, half in (("q", q_half), ("kv", kv_half)):
        for r, ct, tile in tiles_of(kind):
            rows, cols = place(tile)
            here = slice(r * NODES, (r + 1) * NODES), slice(ct * LANE, (ct + 1) * LANE)
            if cols.start < LATE_MSG:
                half[here] = late[rows, cols]
            else:
                half[here] = jnp.zeros((NODES, LANE), BF16)
    q_new[0, 0, 0] = dot(natural_matrix(Q_OWN), q_half[...]).astype(BF16)
    kv_part[...] = dot(natural_matrix(KV_OWN), kv_half[...]).astype(BF16)

    rows, cols = place(PEAK_TILE)
    parts = dot(matrix, arrived_ref[:, cols])
    top, bottom = parts[rows], parts[place(PEAK_TILE + 1)[0]]
    peaks = jnp.max((top[:, :BLOCKS] + top[:, BLOCKS:]) + bottom[:, :BLOCKS], axis=0, keepdims=True)
    diagonal = iota((BLOCKS, BLOCKS), 0) == iota((BLOCKS, BLOCKS), 1)
    peak_col = jnp.sum(jnp.where(diagonal, jnp.broadcast_to(peaks, (BLOCKS, BLOCKS)), 0.0), axis=1, keepdims=True)
    shrink = jnp.minimum(1.0, CLIP_LEVEL / peak_col)
    factor_ref[0] = jnp.broadcast_to(jnp.sqrt(shrink), (BLOCKS, LANE))
    factor_ref[1] = jnp.broadcast_to(shrink, (BLOCKS, LANE))


def settle(late, arrived, q_momentum):
    return call(
        settle_kernel,
        (
            shape((1, 1, 2, Q_ROWS, Q_COLS), BF16),
            pltpu.HBM((KV_ROWS, KV_COLS), BF16),
            shape((2, BLOCKS, LANE), F32),
        ),
        late,
        arrived,
        q_momentum,
        grid=(1,),
        in_specs=[HERE, whole(ROWS, MSG), pl.BlockSpec(memory_space=pl.ANY)],
        out_specs=[
            pl.BlockSpec((1, 1, 1, Q_ROWS, Q_COLS), lambda i: (0, 0, 1, 0, 0)),
            whole(KV_ROWS, KV_COLS),
            whole(2, BLOCKS, LANE),
        ],
        scratch_shapes=[pltpu.VMEM((Q_ROWS, Q_COLS), BF16), pltpu.VMEM((KV_ROWS, KV_COLS), BF16)],
        input_output_aliases={2: 0},
    )


def finish_kernel(
    node_ref, in_ref, matrix_ref, factor_ref, weight_hbm, part_hbm, kv_old, update_hbm, weight_new_hbm, kv_update_ref,
    kv_new_hbm, weight, update, part, kv_new, sems,
):
    fetch = pltpu.make_async_copy(weight_hbm, weight, sems.at[0])
    fetch.start()
    part_fetch = pltpu.make_async_copy(part_hbm, part, sems.at[1])
    part_fetch.start()
    edge = SPLIT * LANE
    q_rows = dot(matrix_ref[0], in_ref[:, : edge + LANE])
    fetch.wait()
    copies = []
    for r in range(Q_OWN):
        factor = jnp.where(node_ref[0] * Q_OWN + r < QN, factor_ref[0], factor_ref[1])
        factor = factor.reshape(LAYERS, PER_GROUP, LANE)
        for ct in range(Q_TILES):
            rows, cols = place(r * Q_TILES + ct)
            lanes = slice(ct * LANE, (ct + 1) * LANE)
            step = q_rows[rows, cols].reshape(LAYERS, PER_GROUP, LANE)
            update[:, r, :, lanes] = step.astype(BF16)
            old = weight[:, r, :, lanes]
            weight[:, r, :, lanes] = (old - LEARN_RATE * (step + DECAY_RATE * old)) * factor
        copies.append(pltpu.make_async_copy(update.at[:, r], update_hbm.at[:, r], sems.at[2 + 2 * r]))
        copies.append(pltpu.make_async_copy(weight.at[:, r], weight_new_hbm.at[:, r], sems.at[3 + 2 * r]))
        copies[-2].start()
        copies[-1].start()
    row, col = iota((KV_TILES * NODES, ROWS), 0), iota((KV_TILES * NODES, ROWS), 1)
    rest_matrix = one(((row & 63) == (col >> 3)) & ((row >> 6) + REST == (col & 7)))
    rest = dot(rest_matrix, in_ref[:, LATE_MSG:]).astype(BF16)
    rest = jnp.concatenate([rest[ct * NODES : (ct + 1) * NODES] for ct in range(KV_TILES)], axis=1)
    spread = one(iota((KV_ROWS, NODES), 0) == iota((KV_ROWS, NODES), 1) * KV_OWN + (KV_OWN - 1))
    part_fetch.wait()
    kv_new[...] = (part[...].astype(F32) + dot(spread, rest)).astype(BF16)
    copies.append(pltpu.make_async_copy(kv_new, kv_new_hbm.at[0, 0, 1], sems.at[2 + 2 * Q_OWN]))
    copies[-1].start()
    kv_rows = dot(matrix_ref[1], in_ref[:, edge:])
    for r, ct, tile in tiles_of("kv"):
        rows, cols = place(tile)
        lanes = slice(cols.start - edge, cols.stop - edge)
        kv_update_ref[r, :, ct * LANE : (ct + 1) * LANE] = kv_rows[rows, lanes].astype(BF16)
    for copy in copies:
        copy.wait()


def finish(node, returned, matrix, factors, weight_query, kv_part, kv_momentum):
    q_dims = (LAYERS, Q_OWN, PER_GROUP, Q_COLS)
    kv_dims = (KV_OWN, BLOCKS, KV_COLS)
    outside = pl.BlockSpec(memory_space=pltpu.HBM)
    return call(
        finish_kernel,
        (
            pltpu.HBM(q_dims, BF16),
            pltpu.HBM(q_dims, F32),
            shape(kv_dims, BF16),
            pltpu.HBM((1, 1, 2, KV_ROWS, KV_COLS), BF16),
        ),
        node,
        returned,
        in_hbm(matrix),
        factors,
        in_hbm(weight_query),
        in_hbm(kv_part),
        in_hbm(kv_momentum),
        grid=(1,),
        in_specs=[
            pl.BlockSpec(memory_space=pltpu.SMEM),
            HERE,
            whole(2, ROWS, ROWS),
            whole(2, BLOCKS, LANE),
            outside,
            outside,
            outside,
        ],
        out_specs=[outside, outside, HERE, outside],
        input_output_aliases={6: 3},
        scratch_shapes=[
            pltpu.VMEM(q_dims, F32),
            pltpu.VMEM(q_dims, BF16),
            pltpu.VMEM((KV_ROWS, KV_COLS), BF16),
            pltpu.VMEM((KV_ROWS, KV_COLS), BF16),
            pltpu.SemaphoreType.DMA((3 + 2 * Q_OWN,)),
        ],
    )


def exchange(message):
    return lax.all_to_all(message, "fsdp", split_axis=0, concat_axis=0, tiled=True)


def on_device(
    grad_query, grad_kv, momentum_query, momentum_kv, weight_query, weight_kv, owner_query, owner_kv, max_logits
):
    my_group = lax.axis_index("dp")
    my_node = lax.axis_index("fsdp")

    node = my_node.astype(I32).reshape(1)
    forward = [(i, (i + 1) % GROUPS) for i in range(GROUPS)]
    backward = [(i, (i + 3) % GROUPS) for i in range(GROUPS)]

    def turn(*steps):
        return (my_group.astype(I32) + jnp.asarray(steps, I32)) % GROUPS

    q_grads = jnp.transpose(grad_query[0], (0, 2, 1, 3))
    kv_grads = jnp.transpose(grad_kv[0], (0, 2, 1, 3))
    peaks = max_logits[0]
    ring_shape = (shape((RING, MSG), BF16),) * 2
    to_next, to_last = arrange_call(first_kernel, turn(2, 1, 3), q_grads, kv_grads, peaks, (), ring_shape)
    to_next, to_last, momentum_query, momentum_kv = lax.optimization_barrier(
        (to_next, to_last, momentum_query, momentum_kv)
    )
    from_last = lax.ppermute(to_next, "dp", forward)
    from_next = lax.ppermute(to_last, "dp", backward)
    late_in = exchange(late_message(momentum_query, momentum_kv))
    table, over, fill = tables(turn(0), owner_query, owner_kv)
    send_matrix, late_back, back_matrix = expand(table)
    hint = pl.CostEstimate(flops=10**12, bytes_accessed=10**10, transcendentals=0)
    to_next, to_last = arrange_call(
        combine_kernel, turn(1, 3), q_grads, kv_grads, peaks, (from_last, from_next),
        ring_shape, hint,
    )
    sum_last = lax.ppermute(to_next, "dp", forward)
    sum_next = lax.ppermute(to_last, "dp", backward)
    (mine,) = arrange_call(mine_kernel, turn(0), q_grads, kv_grads, peaks, (), (pltpu.HBM((ROWS, MSG), BF16),))
    earlier = call(earlier_kernel, shape((ROWS, MSG), BF16), in_hbm(late_in), in_hbm(late_back))

    outside = pl.BlockSpec(memory_space=pltpu.HBM)
    message, carried = call(
        send_kernel,
        (pltpu.HBM((ROWS, MSG), BF16), pltpu.HBM((ROWS, MSG), BF16)),
        mine, sum_last, sum_next, from_last, from_next, earlier, in_hbm(send_matrix), over,
        grid=(1,),
        in_specs=[whole(ROWS, MSG), HERE, HERE] + [pl.BlockSpec((EXTRA, MSG), lambda i: (2, 0))] * 2 + [HERE]
        + [whole(2, ROWS, ROWS), whole(2, BLOCKS, LANE)],
        out_specs=[outside, outside],
        scratch_shapes=[pltpu.VMEM((ROWS, MSG), BF16)] * 3 + [pltpu.SemaphoreType.DMA((3,))],
    )
    late_out, rest = call(
        late_out_kernel, (pltpu.HBM((ROWS, LATE_MSG), BF16), pltpu.HBM((ROWS, LANE), BF16)), carried, table
    )
    arrived, late_out = lax.optimization_barrier((exchange(message), late_out))
    late = exchange(late_out)
    outgoing, q_momentum, kv_momentum = owner_step(node, arrived, momentum_query, momentum_kv, fill, rest)
    late, outgoing = lax.optimization_barrier((late, outgoing))
    returned = exchange(outgoing)
    q_momentum, kv_part, factors = settle(late, arrived, q_momentum)
    q_update, q_weight, kv_update, kv_momentum = finish(
        node, returned, back_matrix, factors, jnp.transpose(weight_query, (0, 2, 1, 3)), kv_part, kv_momentum
    )
    kv_update = jnp.transpose(kv_update.reshape(KV_OWN, LAYERS, PER_GROUP, KV_COLS), (1, 2, 0, 3))
    kv_index = my_node * KV_OWN + jnp.arange(KV_OWN, dtype=I32)
    root_shrink = factors[0, :, 0].reshape(LAYERS, PER_GROUP)
    kv_factor = jnp.where(kv_index[None, None, :, None] < KN, root_shrink[:, :, None, None], 1.0)
    kv_weight = (weight_kv - LEARN_RATE * (kv_update.astype(F32) + DECAY_RATE * weight_kv)) * kv_factor
    return (
        jnp.transpose(q_update, (0, 2, 1, 3)),
        kv_update,
        jnp.transpose(q_weight, (0, 2, 1, 3)),
        kv_weight,
        q_momentum,
        kv_momentum,
    )


def solution(mesh):
    return jax.shard_map(
        on_device,
        mesh=mesh,
        in_specs=(
            P("dp", None, None, "fsdp", None),
            P("dp", None, None, "fsdp", None),
            P("dp", "fsdp", None, None, None),
            P("dp", "fsdp", None, None, None),
            P(None, "dp", "fsdp", None),
            P(None, "dp", "fsdp", None),
            P(),
            P(),
            P(("dp", "fsdp"), None, None),
        ),
        out_specs=(
            P(None, "dp", "fsdp", None),
            P(None, "dp", "fsdp", None),
            P(None, "dp", "fsdp", None),
            P(None, "dp", "fsdp", None),
            P("dp", "fsdp", None, None, None),
            P("dp", "fsdp", None, None, None),
        ),
        check_vma=False,
    )
```

```python
import math

import jax
import jax.numpy as jnp
from jax import lax
from jax.experimental import pallas as pl
from jax.experimental.pallas import tpu as pltpu
from jax.sharding import PartitionSpec as P

QN = 128
KN = 128
STEPS = 5
LAYERS = 4
HEADS = 64
GROUPS = 4
PER_GROUP = 16
NODES = 64
BLOCKS = 64
Q_ROWS, Q_COLS = 192, 1536
KV_ROWS, KV_COLS = 256, 512
Q_OWN, KV_OWN = Q_ROWS // NODES, KV_ROWS // NODES
LANE = 128
Q_TILES, KV_TILES = Q_COLS // LANE, KV_COLS // LANE
SUB = 8
MSG_COLS = 7
MSG = MSG_COLS * LANE
ROWS = NODES * SUB
HALF = ROWS // 2
EXTRA = ROWS // 4
RING = ROWS - EXTRA
PEAK_TILE = Q_OWN * Q_TILES + KV_OWN * KV_TILES
LATE_MSG = MSG - LANE
REST = KV_TILES
SPLIT = Q_OWN * Q_TILES // SUB
SPLIT_SUB = Q_OWN * Q_TILES % SUB

MOMENTUM_RATE = 0.95
LEARN_RATE = 0.02
DECAY_RATE = 0.1
CLIP_LEVEL = 100.0
NEWTON_FIRST = 3.4445
NEWTON_SECOND = -4.775
NEWTON_THIRD = 2.0315
EPSILON = 1e-07
Q_SCALE = 0.2 * math.sqrt(max(Q_ROWS, Q_COLS))
KV_SCALE = 0.2 * math.sqrt(max(KV_ROWS, KV_COLS))

F32 = jnp.float32
BF16 = jnp.bfloat16
I32 = jnp.int32
PARAMS = pltpu.CompilerParams(vmem_limit_bytes=24 * 1024 * 1024)


def place(tile):
    col, sub = divmod(tile, SUB)
    return slice(sub * BLOCKS, (sub + 1) * BLOCKS), slice(col * LANE, (col + 1) * LANE)


def tiles_of(kind):
    if kind == "q":
        return [(r, ct, r * Q_TILES + ct) for r in range(Q_OWN) for ct in range(Q_TILES)]
    base = Q_OWN * Q_TILES
    return [(r, ct, base + r * KV_TILES + ct) for r in range(KV_OWN) for ct in range(KV_TILES)]


def in_hbm(x):
    return pltpu.with_memory_space_constraint(x, pltpu.HBM)


def iota(shape, dim):
    return lax.broadcasted_iota(I32, shape, dim)


def dot(a, b):
    return jnp.dot(a, b, preferred_element_type=F32)


def dot_nt(a, b):
    return lax.dot_general(a, b, (((1,), (1,)), ((), ())), preferred_element_type=F32)


def one(cond):
    return jnp.where(cond, 1.0, 0.0).astype(BF16)


def pack_matrix():
    row, col = iota((ROWS, ROWS), 0), iota((ROWS, ROWS), 1)
    return one(((row >> 3) == (col & 63)) & ((row & 7) == (col >> 6)))


def unpack_matrix():
    row, col = iota((ROWS, ROWS), 0), iota((ROWS, ROWS), 1)
    return one(((row & 63) == (col >> 3)) & ((row >> 6) == (col & 7)))


def natural_matrix(own):
    size = own * NODES
    row, col = iota((size, size), 0), iota((size, size), 1)
    return one(row == (col & 63) * own + (col >> 6))


def split_matrix(own):
    size = own * NODES
    row, col = iota((size, size), 0), iota((size, size), 1)
    return one(col == (row & 63) * own + (row >> 6))


def to_message(q_natural, kv_natural, tiles_ref):
    q_split = dot(split_matrix(Q_OWN), q_natural).astype(BF16)
    kv_split = dot(split_matrix(KV_OWN), kv_natural).astype(BF16)
    tiles_ref[:, SPLIT * LANE :] = jnp.zeros((ROWS, MSG - SPLIT * LANE), BF16)
    for r, ct, tile in tiles_of("q"):
        rows, cols = place(tile)
        tiles_ref[rows, cols] = q_split[r * NODES : (r + 1) * NODES, ct * LANE : (ct + 1) * LANE]
    for r, ct, tile in tiles_of("kv"):
        rows, cols = place(tile)
        tiles_ref[rows, cols] = kv_split[r * NODES : (r + 1) * NODES, ct * LANE : (ct + 1) * LANE]
    return dot(pack_matrix(), tiles_ref[...])


def from_tiles(tiles, q_ref, kv_ref):
    for r, ct, tile in tiles_of("q"):
        rows, cols = place(tile)
        q_ref[r * NODES : (r + 1) * NODES, ct * LANE : (ct + 1) * LANE] = tiles[rows, cols]
    for r, ct, tile in tiles_of("kv"):
        rows, cols = place(tile)
        kv_ref[r * NODES : (r + 1) * NODES, ct * LANE : (ct + 1) * LANE] = tiles[rows, cols]
    return dot(natural_matrix(Q_OWN), q_ref[...]), dot(natural_matrix(KV_OWN), kv_ref[...])


def by_kind(q_matrix, kv_matrix, source, q_rows):
    edge = SPLIT * LANE
    q_part = dot(q_matrix, source[:, : edge + LANE])
    kv_part = dot(kv_matrix, source[:, edge:])
    mixed = jnp.where(q_rows, q_part[:, edge:], kv_part[:, :LANE])
    return jnp.concatenate([q_part[:, :edge], mixed, kv_part[:, LANE:]], axis=1)


def call(kernel, out_shape, *operands, **options):
    return pl.pallas_call(kernel, out_shape=out_shape, compiler_params=PARAMS, **options)(*operands)


def whole(*dims):
    return pl.BlockSpec(dims, lambda i: (0,) * len(dims))


HERE = pl.BlockSpec(memory_space=pltpu.VMEM)


def shape(dims, dtype):
    return jax.ShapeDtypeStruct(dims, dtype)


def parts_of(value):
    high = value.astype(BF16).astype(F32)
    middle = (value - high).astype(BF16).astype(F32)
    return high, middle, (value - high) - middle


def peak_tile(column):
    high, middle, low = parts_of(column)
    lane = iota((column.shape[0], LANE), 1)
    return jnp.where(lane == 0, high, jnp.where(lane == 1, middle, jnp.where(lane == 2, low, 0.0))).astype(BF16)


def peak_column(tile):
    lane = iota(tile.shape, 1)
    return jnp.sum(jnp.where(lane < 3, tile.astype(F32), 0.0), axis=1, keepdims=True)


def group_tiles(group, q_ref, kv_ref, peak_ref, put):
    for tile in range(PEAK_TILE + 1, MSG_COLS * SUB):
        rows, cols = place(tile)
        put(rows.start, cols, jnp.zeros((BLOCKS, LANE), BF16))
    rows, cols = place(PEAK_TILE)
    for layer in range(LAYERS):
        spread = jnp.broadcast_to(peak_ref[layer : layer + 1, :], (PER_GROUP, HEADS))
        mine = iota((PER_GROUP, HEADS), 1) == iota((PER_GROUP, HEADS), 0) + group * PER_GROUP
        column = jnp.sum(jnp.where(mine, spread, 0.0), axis=1, keepdims=True)
        put(rows.start + layer * PER_GROUP, cols, peak_tile(column))
    for kind, ref in (("q", q_ref), ("kv", kv_ref)):
        for r, ct, tile in tiles_of(kind):
            rows, cols = place(tile)
            for layer in range(LAYERS):
                put(rows.start + layer * PER_GROUP, cols, ref[layer, r, :, ct * LANE : (ct + 1) * LANE])


def window(start, size):
    return slice(start, start + size)


def first_kernel(
    group_ref, q_far, kv_far, q_next, kv_next, q_last, kv_last, peak_ref, forward_out, backward_out
):
    def put_far(start, cols, value):
        out = (forward_out, backward_out)[start // HALF]
        out[window(start % HALF, value.shape[0]), cols] = value

    def put_next(start, cols, value):
        if start >= ROWS - EXTRA:
            forward_out[window(start - ROWS + EXTRA + HALF, value.shape[0]), cols] = value

    def put_last(start, cols, value):
        if start < EXTRA:
            backward_out[window(start + HALF, value.shape[0]), cols] = value

    group_tiles(group_ref[0], q_far, kv_far, peak_ref, put_far)
    group_tiles(group_ref[1], q_next, kv_next, peak_ref, put_next)
    group_tiles(group_ref[2], q_last, kv_last, peak_ref, put_last)


def mine_kernel(group_ref, q_ref, kv_ref, peak_ref, out_ref):
    def put(start, cols, value):
        out_ref[window(start, value.shape[0]), cols] = value

    group_tiles(group_ref[0], q_ref, kv_ref, peak_ref, put)


def combine_kernel(
    group_ref, q_next, kv_next, q_last, kv_last, peak_ref, from_last, from_next, next_out, last_out
):
    def put_next(start, cols, value):
        if start >= ROWS - EXTRA:
            return
        if start < HALF:
            value = (value.astype(F32) + from_last[window(start, value.shape[0]), cols].astype(F32)).astype(BF16)
        next_out[window(start, value.shape[0]), cols] = value

    def put_last(start, cols, value):
        if start < EXTRA:
            return
        here = window(start - EXTRA, value.shape[0])
        if start >= HALF:
            far = from_next[window(start - HALF, value.shape[0]), cols]
            if window(start // BLOCKS * BLOCKS, BLOCKS) == peak_rows and cols == peak_cols:
                value = peak_tile(jnp.maximum(peak_column(value), peak_column(far)))
            else:
                value = (value.astype(F32) + far.astype(F32)).astype(BF16)
        last_out[here, cols] = value

    peak_rows, peak_cols = place(PEAK_TILE)
    group_tiles(group_ref[0], q_next, kv_next, peak_ref, put_next)
    group_tiles(group_ref[1], q_last, kv_last, peak_ref, put_last)


def arrange_call(kernel, groups, grad_query, grad_kv, peaks, extra, out_shape, hint=None):
    count = groups.shape[0]

    def at(index):
        return [
            pl.BlockSpec((LAYERS, Q_OWN, PER_GROUP, Q_COLS), lambda i, g: (0, 0, g[index], 0)),
            pl.BlockSpec((LAYERS, KV_OWN, PER_GROUP, KV_COLS), lambda i, g: (0, 0, g[index], 0)),
        ]

    def all_of(x):
        return pl.BlockSpec(x.shape, lambda i, g: (0,) * len(x.shape))

    return pl.pallas_call(
        kernel,
        out_shape=out_shape,
        grid_spec=pltpu.PrefetchScalarGridSpec(
            num_scalar_prefetch=1,
            grid=(1,),
            in_specs=sum([at(index) for index in range(count)], []) + [all_of(peaks)] + [HERE] * len(extra),
            out_specs=[all_of(x) if hint is None and count == 1 else HERE for x in out_shape],
        ),
        compiler_params=PARAMS,
        cost_estimate=hint,
    )(groups, *([in_hbm(grad_query), grad_kv] * count), peaks, *extra)


SEND, LATE, SEND_BACK, LATE_BACK = range(4)


def table_kernel(group_ref, q_ref, kv_ref, table_ref, over_ref, fill_ref):
    group = group_ref[0]
    down, across = iota((NODES, BLOCKS), 0), iota((NODES, BLOCKS), 1)

    def count(cond, axis):
        return jnp.sum(jnp.where(cond, 1.0, 0.0), axis=axis, keepdims=True)

    for kind, ref in enumerate((q_ref, kv_ref)):
        owner_row = jnp.zeros((SUB, BLOCKS), F32)
        for layer in range(LAYERS):
            piece = jnp.broadcast_to(ref[group, layer].astype(F32), (SUB, PER_GROUP)).astype(BF16)
            spot = iota((PER_GROUP, BLOCKS), 1) == iota((PER_GROUP, BLOCKS), 0) + layer * PER_GROUP
            owner_row += dot(piece, one(spot))
        owner_row = owner_row[:1].astype(I32)
        spread = jnp.broadcast_to(owner_row, (BLOCKS, BLOCKS))
        owner_col = jnp.sum(jnp.where(down == across, spread, 0).astype(F32), axis=1, keepdims=True).astype(I32)
        same = owner_col == owner_row
        slot_col = count(same & (across < down), 1)
        slot_row = count(same & (down < across), 0)
        hits = down == owner_row
        hits_back = owner_col == across
        fill_col, fill_row = count(hits, 1), count(hits_back, 0)
        over_col, over_row = slot_col > 0.5, slot_row > 0.5
        free_col, free_row = fill_col < 0.5, fill_row < 0.5
        over_rank_col, over_rank_row = count(over_row & (across < down), 1), count(over_col & (down < across), 0)
        free_rank_col, free_rank_row = count(free_row & (across < down), 1), count(free_col & (down < across), 0)
        table_ref[kind, SEND] = one(
            (hits & ~over_row) | (free_col & over_row & (free_rank_col == over_rank_row))
        )
        table_ref[kind, LATE] = one(hits & over_row)
        table_ref[kind, SEND_BACK] = one(
            (hits_back & ~over_col) | (free_row & over_col & (free_rank_row == over_rank_col))
        )
        table_ref[kind, LATE_BACK] = one(hits_back & over_col)
        over_ref[kind] = jnp.broadcast_to(jnp.where(over_col, 1.0, 0.0), (BLOCKS, LANE))
        fill_ref[kind] = jnp.broadcast_to(fill_col, (BLOCKS, LANE))


def tables(group, owner_query, owner_kv):
    return call(
        table_kernel,
        (shape((2, 4, NODES, BLOCKS), BF16), shape((2, BLOCKS, LANE), F32), shape((2, NODES, LANE), F32)),
        group,
        jnp.transpose(owner_query, (0, 1, 3, 2)),
        jnp.transpose(owner_kv, (0, 1, 3, 2)),
        in_specs=[pl.BlockSpec(memory_space=pltpu.SMEM)] + [pl.BlockSpec(memory_space=pltpu.VMEM)] * 2,
    )


def to_peers(table):
    rows = one((iota((ROWS, NODES), 0) >> 3) == iota((ROWS, NODES), 1))
    cols = one(iota((BLOCKS, ROWS), 0) == (iota((BLOCKS, ROWS), 1) & 63))
    wide = dot(dot(rows, table).astype(BF16), cols)
    row, col = iota((ROWS, ROWS), 0), iota((ROWS, ROWS), 1)
    return jnp.where((row & 7) == (col >> 6), wide, 0.0).astype(BF16)


def to_tiles(table):
    rows = one((iota((ROWS, BLOCKS), 0) & 63) == iota((ROWS, BLOCKS), 1))
    cols = one(iota((NODES, ROWS), 0) == (iota((NODES, ROWS), 1) >> 3))
    wide = dot(dot(rows, table).astype(BF16), cols)
    row, col = iota((ROWS, ROWS), 0), iota((ROWS, ROWS), 1)
    return jnp.where((row >> 6) == (col & 7), wide, 0.0).astype(BF16)


def expand_kernel(table_ref, send_ref, late_back_ref, back_ref):
    for kind in range(2):
        send_ref[kind] = to_peers(table_ref[kind, SEND])
        late_back_ref[kind] = to_tiles(table_ref[kind, LATE_BACK])
        back_ref[kind] = to_tiles(table_ref[kind, SEND_BACK])


def expand(table):
    return call(expand_kernel, (pltpu.HBM((2, ROWS, ROWS), BF16),) * 3, table)


def late_kernel(q_ref, kv_ref, out_ref, tiles_ref):
    out_ref[...] = to_message(q_ref[0, 0, 0], kv_ref[0, 0, 0], tiles_ref).astype(BF16)


def late_message(momentum_query, momentum_kv):
    return call(
        late_kernel,
        pltpu.HBM((ROWS, MSG), BF16),
        in_hbm(momentum_query),
        in_hbm(momentum_kv),
        grid=(1,),
        in_specs=[
            pl.BlockSpec((1, 1, 1, Q_ROWS, Q_COLS), lambda i: (0, 0, 1, 0, 0)),
            pl.BlockSpec((1, 1, 1, KV_ROWS, KV_COLS), lambda i: (0, 0, 1, 0, 0)),
        ],
        out_specs=pl.BlockSpec((ROWS, MSG), lambda i: (0, 0)),
        scratch_shapes=[pltpu.VMEM((ROWS, MSG), BF16)],
    )


def earlier_kernel(late_in_ref, matrix_ref, out_ref):
    tile_rows = iota((ROWS, LANE), 0) < SPLIT_SUB * BLOCKS
    out_ref[...] = by_kind(matrix_ref[0], matrix_ref[1], late_in_ref[...], tile_rows).astype(BF16)


def send_kernel(
    mine_ref, last_ref, next_ref, first_last, first_next, earlier_ref, matrix_ref, over_ref, out_hbm, carried_hbm,
    chosen, carried, message, sems,
):
    row = iota((ROWS, LANE), 0)
    q_over = jnp.concatenate([over_ref[0]] * SUB, axis=0)
    kv_over = jnp.concatenate([over_ref[1]] * SUB, axis=0)
    for col in range(MSG_COLS):
        lanes = slice(col * LANE, (col + 1) * LANE)
        last = jnp.concatenate([last_ref[:, lanes], first_last[:, lanes]], axis=0).astype(F32)
        following = jnp.concatenate([first_next[:, lanes], next_ref[:, lanes]], axis=0).astype(F32)
        reduced = mine_ref[:, lanes].astype(F32) + (last + following)
        reduced = reduced.astype(BF16).astype(F32)
        moved = MOMENTUM_RATE * earlier_ref[:, lanes].astype(F32) + reduced
        carried[:, lanes] = moved.astype(BF16)
        if col < SPLIT:
            mask = q_over
        elif col == SPLIT:
            mask = jnp.where(row < SPLIT_SUB * BLOCKS, q_over, kv_over)
        else:
            mask = kv_over
        chosen[:, lanes] = jnp.where(mask > 0.5, reduced + MOMENTUM_RATE * moved, reduced).astype(BF16)
    carried_copy = pltpu.make_async_copy(carried, carried_hbm, sems.at[0])
    carried_copy.start()
    edge = SPLIT * LANE
    q_part = dot(matrix_ref[0], chosen[:, : edge + LANE])
    message[:, :edge] = q_part[:, :edge].astype(BF16)
    q_copy = pltpu.make_async_copy(message.at[:, :edge], out_hbm.at[:, :edge], sems.at[1])
    q_copy.start()
    kv_part = dot(matrix_ref[1], chosen[:, edge:])
    peer_rows = (row & 7) < SPLIT_SUB
    message[:, edge : edge + LANE] = jnp.where(peer_rows, q_part[:, edge:], kv_part[:, :LANE]).astype(BF16)
    rows, cols = place(PEAK_TILE)
    peak = jnp.maximum(peak_column(mine_ref[rows, cols]), peak_column(last_ref[rows, cols]))
    peak = jnp.maximum(peak, peak_column(next_ref[rows.start - EXTRA : rows.stop - EXTRA, cols]))
    spot = iota((BLOCKS, LANE), 0) == (iota((BLOCKS, LANE), 1) & 63)
    peak = jnp.sum(jnp.where(spot, jnp.broadcast_to(peak, (BLOCKS, LANE)), 0.0), axis=0, keepdims=True)
    high, middle, low = parts_of(peak)
    sub = PEAK_TILE % SUB
    first_half = iota((ROWS, LANE), 1) < LANE // 2
    last = kv_part[:, cols.start - edge :]
    last = jnp.where((row & 7) == sub, jnp.where(first_half, high, middle), last)
    last = jnp.where((row & 7) == sub + 1, jnp.where(first_half, low, 0.0), last)
    message[:, edge + LANE : cols.start] = kv_part[:, LANE : cols.start - edge].astype(BF16)
    message[:, cols] = last.astype(BF16)
    kv_copy = pltpu.make_async_copy(message.at[:, edge:], out_hbm.at[:, edge:], sems.at[2])
    kv_copy.start()
    carried_copy.wait()
    q_copy.wait()
    kv_copy.wait()


def late_out_kernel(carried_ref, table_ref, out_ref, rest_ref):
    row = iota((ROWS, LANE), 0)
    q_matrix, kv_matrix = to_peers(table_ref[0, LATE]), to_peers(table_ref[1, LATE])
    placed = by_kind(q_matrix, kv_matrix, carried_ref[...], (row & 7) < SPLIT_SUB)
    out_ref[...] = placed[:, :LATE_MSG].astype(BF16)
    moved = pltpu.roll(placed[:, LATE_MSG:], REST, 0)
    rest_ref[...] = jnp.where((row & 7) >= REST, moved, 0.0).astype(BF16)


def halves(x):
    high = x.astype(BF16)
    return high, (x - high.astype(F32)).astype(BF16)


def product(a, b, op):
    size = a[0].shape[0]
    both = op(jnp.concatenate(a, axis=0), b[0])
    return both[:size] + (both[size:] + op(a[0], b[1]))


def newton_step(refs):
    values = [ref[...] for ref in refs]
    parts = [halves(x) for x in values]
    squares = [product(h, h, dot_nt) for h in parts]
    square_parts = [halves(square) for square in squares]
    polynomials = [
        NEWTON_SECOND * square + NEWTON_THIRD * product(h, h, dot) for square, h in zip(squares, square_parts)
    ]
    for ref, x, h, polynomial in zip(refs, values, parts, polynomials):
        ref[...] = NEWTON_FIRST * x + product(halves(polynomial), h, dot)


def owner_kernel(
    node_ref, in_ref, q_mom, kv_mom, fill_ref, rest_ref, out_ref, q_new, kv_new, q_x, kv_x, q_half, kv_half, tiles_ref
):
    node = node_ref[0]
    received = dot(unpack_matrix(), in_ref[...])
    arrived = from_tiles(received.astype(BF16), q_half, kv_half)
    for kind, gradient, mom, new, x_ref in (
        (0, arrived[0], q_mom, q_new, q_x),
        (1, arrived[1], kv_mom, kv_new, kv_x),
    ):
        used = fill_ref[kind, pl.ds(node, 1), :1] > 0.5
        carried = MOMENTUM_RATE * mom[0, 0, 0].astype(F32) + gradient
        new[0, 0, 0] = jnp.where(used, carried, 0.0).astype(BF16)
        direction = jnp.where(used, gradient + MOMENTUM_RATE * carried, gradient)
        norm = jnp.sqrt(jnp.sum(direction * direction)) + EPSILON
        x_ref[...] = direction / norm

    def body(_, carry):
        newton_step((q_x, kv_x))
        return carry

    lax.fori_loop(0, STEPS, body, 0)
    outgoing = to_message((q_x[...] * Q_SCALE).astype(BF16), (kv_x[...] * KV_SCALE).astype(BF16), tiles_ref)
    out_ref[:, :LATE_MSG] = outgoing[:, :LATE_MSG].astype(BF16)
    out_ref[:, LATE_MSG:] = (outgoing[:, LATE_MSG:] + rest_ref[...].astype(F32)).astype(BF16)


def owner_step(node, arrived, momentum_query, momentum_kv, fill, rest):
    q_slot = pl.BlockSpec((1, 1, 1, Q_ROWS, Q_COLS), lambda i: (0, 0, 0, 0, 0))
    kv_slot = pl.BlockSpec((1, 1, 1, KV_ROWS, KV_COLS), lambda i: (0, 0, 0, 0, 0))
    return call(
        owner_kernel,
        (
            pltpu.HBM((ROWS, MSG), BF16),
            pltpu.HBM((1, 1, 2, Q_ROWS, Q_COLS), BF16),
            pltpu.HBM((1, 1, 2, KV_ROWS, KV_COLS), BF16),
        ),
        node,
        arrived,
        in_hbm(momentum_query),
        in_hbm(momentum_kv),
        fill,
        in_hbm(rest),
        grid=(1,),
        in_specs=[pl.BlockSpec(memory_space=pltpu.SMEM), HERE, q_slot, kv_slot, whole(2, NODES, LANE), whole(ROWS, LANE)],
        out_specs=[whole(ROWS, MSG), q_slot, kv_slot],
        scratch_shapes=[
            pltpu.VMEM((Q_ROWS, Q_COLS), F32),
            pltpu.VMEM((KV_ROWS, KV_COLS), F32),
            pltpu.VMEM((Q_ROWS, Q_COLS), BF16),
            pltpu.VMEM((KV_ROWS, KV_COLS), BF16),
            pltpu.VMEM((ROWS, MSG), BF16),
        ],
    )


def settle_kernel(in_ref, arrived_ref, q_old, q_new, kv_part, factor_ref, q_half, kv_half):
    matrix = unpack_matrix()
    late = dot(matrix, in_ref[...]).astype(BF16)
    for kind, half in (("q", q_half), ("kv", kv_half)):
        for r, ct, tile in tiles_of(kind):
            rows, cols = place(tile)
            here = slice(r * NODES, (r + 1) * NODES), slice(ct * LANE, (ct + 1) * LANE)
            if cols.start < LATE_MSG:
                half[here] = late[rows, cols]
            else:
                half[here] = jnp.zeros((NODES, LANE), BF16)
    q_new[0, 0, 0] = dot(natural_matrix(Q_OWN), q_half[...]).astype(BF16)
    kv_part[...] = dot(natural_matrix(KV_OWN), kv_half[...]).astype(BF16)

    rows, cols = place(PEAK_TILE)
    parts = dot(matrix, arrived_ref[:, cols])
    top, bottom = parts[rows], parts[place(PEAK_TILE + 1)[0]]
    peaks = jnp.max((top[:, :BLOCKS] + top[:, BLOCKS:]) + bottom[:, :BLOCKS], axis=0, keepdims=True)
    diagonal = iota((BLOCKS, BLOCKS), 0) == iota((BLOCKS, BLOCKS), 1)
    peak_col = jnp.sum(jnp.where(diagonal, jnp.broadcast_to(peaks, (BLOCKS, BLOCKS)), 0.0), axis=1, keepdims=True)
    shrink = jnp.minimum(1.0, CLIP_LEVEL / peak_col)
    factor_ref[0] = jnp.broadcast_to(jnp.sqrt(shrink), (BLOCKS, LANE))
    factor_ref[1] = jnp.broadcast_to(shrink, (BLOCKS, LANE))


def settle(late, arrived, q_momentum):
    return call(
        settle_kernel,
        (
            shape((1, 1, 2, Q_ROWS, Q_COLS), BF16),
            pltpu.HBM((KV_ROWS, KV_COLS), BF16),
            shape((2, BLOCKS, LANE), F32),
        ),
        late,
        arrived,
        q_momentum,
        grid=(1,),
        in_specs=[HERE, whole(ROWS, MSG), pl.BlockSpec(memory_space=pl.ANY)],
        out_specs=[
            pl.BlockSpec((1, 1, 1, Q_ROWS, Q_COLS), lambda i: (0, 0, 1, 0, 0)),
            whole(KV_ROWS, KV_COLS),
            whole(2, BLOCKS, LANE),
        ],
        scratch_shapes=[pltpu.VMEM((Q_ROWS, Q_COLS), BF16), pltpu.VMEM((KV_ROWS, KV_COLS), BF16)],
        input_output_aliases={2: 0},
    )


def finish_kernel(
    node_ref, in_ref, matrix_hbm, factor_ref, weight_hbm, part_hbm, kv_old, update_hbm, weight_new_hbm, kv_update_ref,
    kv_new_hbm, weight, update, part, kv_new, matrix_ref, sems,
):
    matrices = [
        pltpu.make_async_copy(matrix_hbm.at[kind], matrix_ref.at[kind], sems.at[3 + 2 * Q_OWN + kind]) for kind in range(2)
    ]
    matrices[0].start()
    fetch = pltpu.make_async_copy(weight_hbm, weight, sems.at[0])
    fetch.start()
    matrices[1].start()
    part_fetch = pltpu.make_async_copy(part_hbm, part, sems.at[1])
    part_fetch.start()
    edge = SPLIT * LANE
    matrices[0].wait()
    q_rows = dot(matrix_ref[0], in_ref[:, : edge + LANE])
    fetch.wait()
    copies = []
    for r in range(Q_OWN):
        factor = jnp.where(node_ref[0] * Q_OWN + r < QN, factor_ref[0], factor_ref[1])
        factor = factor.reshape(LAYERS, PER_GROUP, LANE)
        for ct in range(Q_TILES):
            rows, cols = place(r * Q_TILES + ct)
            lanes = slice(ct * LANE, (ct + 1) * LANE)
            step = q_rows[rows, cols].reshape(LAYERS, PER_GROUP, LANE)
            update[:, r, :, lanes] = step.astype(BF16)
            old = weight[:, r, :, lanes]
            weight[:, r, :, lanes] = (old - LEARN_RATE * (step + DECAY_RATE * old)) * factor
        copies.append(pltpu.make_async_copy(update.at[:, r], update_hbm.at[:, r], sems.at[2 + 2 * r]))
        copies.append(pltpu.make_async_copy(weight.at[:, r], weight_new_hbm.at[:, r], sems.at[3 + 2 * r]))
        copies[-2].start()
        copies[-1].start()
    row, col = iota((KV_TILES * NODES, ROWS), 0), iota((KV_TILES * NODES, ROWS), 1)
    rest_matrix = one(((row & 63) == (col >> 3)) & ((row >> 6) + REST == (col & 7)))
    rest = dot(rest_matrix, in_ref[:, LATE_MSG:]).astype(BF16)
    rest = jnp.concatenate([rest[ct * NODES : (ct + 1) * NODES] for ct in range(KV_TILES)], axis=1)
    spread = one(iota((KV_ROWS, NODES), 0) == iota((KV_ROWS, NODES), 1) * KV_OWN + (KV_OWN - 1))
    part_fetch.wait()
    kv_new[...] = (part[...].astype(F32) + dot(spread, rest)).astype(BF16)
    copies.append(pltpu.make_async_copy(kv_new, kv_new_hbm.at[0, 0, 1], sems.at[2 + 2 * Q_OWN]))
    copies[-1].start()
    matrices[1].wait()
    kv_rows = dot(matrix_ref[1], in_ref[:, edge:])
    for r, ct, tile in tiles_of("kv"):
        rows, cols = place(tile)
        lanes = slice(cols.start - edge, cols.stop - edge)
        kv_update_ref[r, :, ct * LANE : (ct + 1) * LANE] = kv_rows[rows, lanes].astype(BF16)
    for copy in copies:
        copy.wait()


def finish(node, returned, matrix, factors, weight_query, kv_part, kv_momentum):
    q_dims = (LAYERS, Q_OWN, PER_GROUP, Q_COLS)
    kv_dims = (KV_OWN, BLOCKS, KV_COLS)
    outside = pl.BlockSpec(memory_space=pltpu.HBM)
    return call(
        finish_kernel,
        (
            pltpu.HBM(q_dims, BF16),
            pltpu.HBM(q_dims, F32),
            shape(kv_dims, BF16),
            pltpu.HBM((1, 1, 2, KV_ROWS, KV_COLS), BF16),
        ),
        node,
        returned,
        in_hbm(matrix),
        factors,
        in_hbm(weight_query),
        in_hbm(kv_part),
        in_hbm(kv_momentum),
        grid=(1,),
        in_specs=[
            pl.BlockSpec(memory_space=pltpu.SMEM),
            HERE,
            outside,
            whole(2, BLOCKS, LANE),
            outside,
            outside,
            outside,
        ],
        out_specs=[outside, outside, HERE, outside],
        input_output_aliases={6: 3},
        scratch_shapes=[
            pltpu.VMEM(q_dims, F32),
            pltpu.VMEM(q_dims, BF16),
            pltpu.VMEM((KV_ROWS, KV_COLS), BF16),
            pltpu.VMEM((KV_ROWS, KV_COLS), BF16),
            pltpu.VMEM((2, ROWS, ROWS), BF16),
            pltpu.SemaphoreType.DMA((5 + 2 * Q_OWN,)),
        ],
    )


def exchange(message):
    return lax.all_to_all(message, "fsdp", split_axis=0, concat_axis=0, tiled=True)


def on_device(
    grad_query, grad_kv, momentum_query, momentum_kv, weight_query, weight_kv, owner_query, owner_kv, max_logits
):
    my_group = lax.axis_index("dp")
    my_node = lax.axis_index("fsdp")

    node = my_node.astype(I32).reshape(1)
    forward = [(i, (i + 1) % GROUPS) for i in range(GROUPS)]
    backward = [(i, (i + 3) % GROUPS) for i in range(GROUPS)]

    def turn(*steps):
        return (my_group.astype(I32) + jnp.asarray(steps, I32)) % GROUPS

    q_grads = jnp.transpose(grad_query[0], (0, 2, 1, 3))
    kv_grads = jnp.transpose(grad_kv[0], (0, 2, 1, 3))
    peaks = max_logits[0]
    ring_shape = (shape((RING, MSG), BF16),) * 2
    to_next, to_last = arrange_call(first_kernel, turn(2, 1, 3), q_grads, kv_grads, peaks, (), ring_shape)
    to_next, to_last, momentum_query, momentum_kv = lax.optimization_barrier(
        (to_next, to_last, momentum_query, momentum_kv)
    )
    from_last = lax.ppermute(to_next, "dp", forward)
    from_next = lax.ppermute(to_last, "dp", backward)
    late_in = exchange(late_message(momentum_query, momentum_kv))
    table, over, fill = tables(turn(0), owner_query, owner_kv)
    send_matrix, late_back, back_matrix = expand(table)
    hint = pl.CostEstimate(flops=10**12, bytes_accessed=10**10, transcendentals=0)
    to_next, to_last = arrange_call(
        combine_kernel, turn(1, 3), q_grads, kv_grads, peaks, (from_last, from_next),
        ring_shape, hint,
    )
    sum_last = lax.ppermute(to_next, "dp", forward)
    sum_next = lax.ppermute(to_last, "dp", backward)
    (mine,) = arrange_call(mine_kernel, turn(0), q_grads, kv_grads, peaks, (), (pltpu.HBM((ROWS, MSG), BF16),))
    earlier = call(
        earlier_kernel, shape((ROWS, MSG), BF16), late_in, in_hbm(late_back),
        in_specs=[HERE, HERE], out_specs=HERE,
    )

    outside = pl.BlockSpec(memory_space=pltpu.HBM)
    message, carried = call(
        send_kernel,
        (pltpu.HBM((ROWS, MSG), BF16), pltpu.HBM((ROWS, MSG), BF16)),
        mine, sum_last, sum_next, from_last, from_next, earlier, in_hbm(send_matrix), over,
        grid=(1,),
        in_specs=[whole(ROWS, MSG), HERE, HERE] + [pl.BlockSpec((EXTRA, MSG), lambda i: (2, 0))] * 2 + [HERE]
        + [whole(2, ROWS, ROWS), whole(2, BLOCKS, LANE)],
        out_specs=[outside, outside],
        scratch_shapes=[pltpu.VMEM((ROWS, MSG), BF16)] * 3 + [pltpu.SemaphoreType.DMA((3,))],
    )
    late_out, rest = call(
        late_out_kernel, (pltpu.HBM((ROWS, LATE_MSG), BF16), pltpu.HBM((ROWS, LANE), BF16)), carried, table
    )
    arrived, late_out = lax.optimization_barrier((exchange(message), late_out))
    late = exchange(late_out)
    outgoing, q_momentum, kv_momentum = owner_step(node, arrived, momentum_query, momentum_kv, fill, rest)
    late, outgoing = lax.optimization_barrier((late, outgoing))
    returned = exchange(outgoing)
    q_momentum, kv_part, factors = settle(late, arrived, q_momentum)
    q_update, q_weight, kv_update, kv_momentum = finish(
        node, returned, back_matrix, factors, jnp.transpose(weight_query, (0, 2, 1, 3)), kv_part, kv_momentum
    )
    kv_update = jnp.transpose(kv_update.reshape(KV_OWN, LAYERS, PER_GROUP, KV_COLS), (1, 2, 0, 3))
    kv_index = my_node * KV_OWN + jnp.arange(KV_OWN, dtype=I32)
    root_shrink = factors[0, :, 0].reshape(LAYERS, PER_GROUP)
    kv_factor = jnp.where(kv_index[None, None, :, None] < KN, root_shrink[:, :, None, None], 1.0)
    kv_weight = (weight_kv - LEARN_RATE * (kv_update.astype(F32) + DECAY_RATE * weight_kv)) * kv_factor
    return (
        jnp.transpose(q_update, (0, 2, 1, 3)),
        kv_update,
        jnp.transpose(q_weight, (0, 2, 1, 3)),
        kv_weight,
        q_momentum,
        kv_momentum,
    )


def solution(mesh):
    return jax.shard_map(
        on_device,
        mesh=mesh,
        in_specs=(
            P("dp", None, None, "fsdp", None),
            P("dp", None, None, "fsdp", None),
            P("dp", "fsdp", None, None, None),
            P("dp", "fsdp", None, None, None),
            P(None, "dp", "fsdp", None),
            P(None, "dp", "fsdp", None),
            P(),
            P(),
            P(("dp", "fsdp"), None, None),
        ),
        out_specs=(
            P(None, "dp", "fsdp", None),
            P(None, "dp", "fsdp", None),
            P(None, "dp", "fsdp", None),
            P(None, "dp", "fsdp", None),
            P("dp", "fsdp", None, None, None),
            P("dp", "fsdp", None, None, None),
        ),
        check_vma=False,
    )
```
